32 devices in a mesh: expert: 8 (over z, y), dp: 4 (over x, core).
Axes of the slice: x: 2, y: 2, z: 4, core: 2. Of those that a mesh axis runs over, the one named last changes fastest.
Arguments:
- tokens: bfloat16 [1024, 3584], P('expert', 'dp'), may hold values from -6 to 6
- expert_ids: int32 [1024, 8], P('expert'), may hold values from 0 to 15, as said below
- gate_weights: float32 [1024, 8], P('expert'), may hold values from 0.05 to 0.5
- replica_plan: int32 [8], replicated, may hold values from 0 to 15, as said below
- w_gate: bfloat16 [16, 3584, 1024], P('expert', None, 'dp'), may hold values from -0.09375 to 0.09375
- w_up: bfloat16 [16, 3584, 1024], P('expert', None, 'dp'), may hold values from -0.09375 to 0.09375
- w_down: bfloat16 [16, 1024, 3584], P('expert', 'dp'), may hold values from -0.1875 to 0.1875
Outputs:
- mixed_out: bfloat16 [1024, 3584], P('expert', 'dp')
The draws below stay inside these ranges and needn't reach their ends.
Inputs may be any that keep to these rules, and one draw needn't show every extreme that they name: `expert_ids`: each row names 8 different experts; one expert, which varies with the draw, is named by every row. `replica_plan`: entry j names one of the 2 experts owned by index (j + 4) % 8 of the expert axis, that is, an expert from k * 2 to k * 2 + 1 with that index k.
All inputs are finite; a program needn't handle non-finite values.
Results may differ from the reference program's by a relative error of at most 0.012.
Values may be sent and summed in bfloat16 or wider, within the bound.
No kernel may reach another device: no remote copies, remote signals or barrier semaphores. Data moves between devices by JAX's collectives and lax.ppermute only.
A program may use at most 128 MiB of HBM per device.

```python
import math
import jax
import jax.numpy as jnp
from jax import lax

D = 3584
FF = 1024
EXP_DEV = 2
TOP = 8
CAP = 8
TOK_DEV = 128
OWNERS = 8
EXPERTS = 16
TOKENS = 1024
N_DP = 4


def hot_levels(key):
    shuffled = jax.random.permutation(jax.random.fold_in(key, 11), EXPERTS)
    position = jnp.zeros((EXPERTS,), jnp.int32).at[shuffled].set(jnp.arange(EXPERTS, dtype=jnp.int32))
    levels = jnp.where(position == 0, 64, jnp.where(position <= EXPERTS // 8, 2, jnp.where(position <= EXPERTS // 4, 1, 0)))
    return levels.astype(jnp.int32)


def draw_expert_ids(key, part):
    levels = hot_levels(key)
    noise_bits = jax.random.randint(jax.random.fold_in(key, 23), (TOKENS, EXPERTS), 0, 65536)
    scores = (noise_bits + levels[None, :] * 4096) * EXPERTS + jnp.arange(EXPERTS, dtype=jnp.int32)[None, :]
    return lax.top_k(scores, TOP)[1].astype(jnp.int32)


def draw_replica_plan(key, part):
    levels = hot_levels(key)
    owner_index = (jnp.arange(OWNERS, dtype=jnp.int32) + OWNERS // 2) % OWNERS
    candidate = owner_index[:, None] * EXP_DEV + jnp.arange(EXP_DEV, dtype=jnp.int32)[None, :]
    tiebreak = jax.random.randint(jax.random.fold_in(key, 31), (OWNERS, EXP_DEV), 0, 1024)
    scores = (levels[candidate] * 1024 + tiebreak) * EXP_DEV + jnp.arange(EXP_DEV, dtype=jnp.int32)[None, :]
    chosen = lax.top_k(scores, 1)[1][:, 0]
    return (owner_index * EXP_DEV + chosen).astype(jnp.int32)


def block_scale(rng, shape, split, smallest, largest):
    loudness, own = 1.0, jax.random.fold_in(rng, 6)
    for dim, blocks in split:
        heights = jnp.exp(jax.random.uniform(jax.random.fold_in(own, dim), (blocks,), jnp.float32, smallest / len(split), largest / len(split)))
        loudness = loudness * jnp.repeat(heights, shape[dim] // blocks).reshape([-1 if axis == dim else 1 for axis in range(len(shape))])
    return loudness


def bell_draw(key, dims, spread, limit, split=(), kind=jnp.bfloat16):
    result = jax.random.normal(key, dims, jnp.float32) * spread
    if len(split) > 0:
        result = block_scale(key, dims, split, -0.22, 0.18) * result
    return jnp.clip(result, min=-limit, max=limit).astype(kind)


def setup_inputs(seed: int = 0) -> dict:
    keys = jax.random.split(jax.random.key(seed), 8)
    return {
        "tokens": bell_draw(keys[0], (TOKENS, D), 1.0, 6.0, ((0, 8), (1, 4))),
        "expert_ids": draw_expert_ids(jax.random.fold_in(keys[7], 71), 0),
        "gate_weights": jnp.clip(jnp.exp(math.log(0.5) - 2.3025851 * jax.random.uniform(keys[2], (TOKENS, TOP), jnp.float32) ** block_scale(keys[2], (TOKENS, TOP), ((0, 8),), -0.2, 0.2)), 0.05, 0.5),
        "replica_plan": draw_replica_plan(jax.random.fold_in(keys[7], 71), 0),
        "w_gate": bell_draw(keys[4], (EXPERTS, D, FF), D ** -0.5, 0.09375, ((0, 8), (2, 4))),
        "w_up": bell_draw(keys[5], (EXPERTS, D, FF), D ** -0.5, 0.09375, ((0, 8), (2, 4))),
        "w_down": bell_draw(keys[6], (EXPERTS, FF, D), FF ** -0.5, 0.1875, ((0, 8), (1, 4))),
    }


def routing_tables(expert_ids, gate_weights, replica_plan):
    host_slots = EXP_DEV + 1
    per_block = TOK_DEV * TOP
    block_ids = expert_ids.reshape(OWNERS, per_block)
    expert_range = jnp.arange(EXPERTS, dtype=jnp.int32)
    onehot = (block_ids[:, :, None] == expert_range[None, None, :]).astype(jnp.int32)
    row_rank = jnp.sum((jnp.cumsum(onehot, axis=1) - onehot) * onehot, axis=2)
    hosted = (replica_plan[:, None] == expert_range[None, :]).astype(jnp.int32)
    copies = 1 + jnp.sum(hosted, axis=0)
    host_of = jnp.sum(jnp.arange(OWNERS, dtype=jnp.int32)[:, None] * hosted, axis=0)
    my_copies = copies[block_ids]
    my_host = host_of[block_ids]
    copy_index = row_rank % my_copies
    position = row_rank // my_copies
    is_kept = position < CAP
    target = jnp.where(copy_index == 0, block_ids // EXP_DEV, my_host)
    target_slot = jnp.where(copy_index == 0, block_ids % EXP_DEV, EXP_DEV)
    sender = jnp.arange(OWNERS, dtype=jnp.int32)[:, None]
    buffer_rows = OWNERS * host_slots * OWNERS * CAP
    slot_place = jnp.where(is_kept, ((target * host_slots + target_slot) * OWNERS + sender) * CAP + position, buffer_rows)
    token_row = sender * TOK_DEV + jnp.arange(per_block, dtype=jnp.int32)[None, :] // TOP
    table = jnp.full((buffer_rows,), TOKENS, jnp.int32).at[slot_place.reshape(-1)].set(token_row.reshape(-1), mode="drop")
    weight_table = jnp.zeros((buffer_rows,), jnp.float32).at[slot_place.reshape(-1)].set(gate_weights.reshape(-1), mode="drop")
    return table, weight_table


def expert_rows(slot_rows, expert, w_gate, w_up, w_down):
    quarter = FF // N_DP
    gate_full = w_gate[expert]
    up_full = w_up[expert]
    down_full = w_down[expert]
    running = jnp.zeros((slot_rows.shape[0], D), jnp.float32)
    for part_number in range(N_DP):
        start_col = part_number * quarter
        stop_col = start_col + quarter
        gate_value = jnp.dot(slot_rows, gate_full[:, start_col:stop_col], preferred_element_type=jnp.float32)
        up_value = jnp.dot(slot_rows, up_full[:, start_col:stop_col], preferred_element_type=jnp.float32)
        hidden = (jax.nn.silu(gate_value) * up_value).astype(jnp.bfloat16)
        partial_value = jnp.dot(hidden, down_full[start_col:stop_col, :], preferred_element_type=jnp.float32).astype(jnp.bfloat16)
        partial_value = lax.optimization_barrier(partial_value)
        running = running + partial_value.astype(jnp.float32)
    return running


def reference(tokens, expert_ids, gate_weights, replica_plan, w_gate, w_up, w_down):
    table, weight_table = routing_tables(expert_ids, gate_weights, replica_plan)
    host_slots = EXP_DEV + 1
    padded = jnp.concatenate([tokens, jnp.zeros((1, D), tokens.dtype)], axis=0)
    owned = jnp.arange(OWNERS, dtype=jnp.int32)[:, None] * EXP_DEV + jnp.arange(EXP_DEV, dtype=jnp.int32)[None, :]
    slot_expert = jnp.concatenate([owned, replica_plan[:, None]], axis=1).reshape(-1)
    slot_tables = table.reshape(OWNERS * host_slots, OWNERS * CAP)
    slot_weights = weight_table.reshape(OWNERS * host_slots, OWNERS * CAP)

    def visit(running, inputs):
        rows_index, row_weights, expert = inputs
        values = expert_rows(padded[rows_index], expert, w_gate, w_up, w_down)
        return running.at[rows_index].add(values * row_weights[:, None]), None

    start = jnp.zeros((TOKENS + 1, D), jnp.float32)
    mixed_out, unused = lax.scan(visit, start, (slot_tables, slot_weights, slot_expert))
    return mixed_out[:TOKENS].astype(jnp.bfloat16)
```

```python
import functools

import jax
import jax.numpy as jnp
from jax import lax
from jax.experimental import pallas as pl
from jax.experimental.pallas import tpu as pltpu
from jax.sharding import PartitionSpec as P

CAP = 8
F32 = jnp.float32
BF16 = jnp.bfloat16
VMEM = pl.BlockSpec(memory_space=pltpu.VMEM)
SMEM = pl.BlockSpec(memory_space=pltpu.SMEM)
LIMIT = 40 * 2**20


def dot(left, right):
    return jnp.dot(left, right, preferred_element_type=F32)


def dot_rows(left, right, precision=None):
    return lax.dot_general(
        left, right, (((0,), (0,)), ((), ())), precision=precision, preferred_element_type=F32
    )


def route_kernel(owned, plan, ids, gates, tokens, outgoing, mix_high, mix_low):
    tok_rows, choices = ids.shape
    share = tokens.shape[1]
    owners = plan.shape[0]
    experts = owners * owned
    row = lax.broadcasted_iota(jnp.int32, (tok_rows, tok_rows), 0)
    col = lax.broadcasted_iota(jnp.int32, (tok_rows, tok_rows), 1)
    same = (row == col).astype(F32)
    earlier = (row < col).astype(BF16)
    ids_t = dot_rows(ids[...].astype(F32).astype(BF16), same.astype(BF16)).astype(jnp.int32)
    gates_t = dot_rows(gates[...], same, lax.Precision.HIGHEST)
    expert = lax.broadcasted_iota(jnp.int32, (experts, tok_rows), 0)
    named = jnp.zeros((experts, tok_rows), F32)
    weight = jnp.zeros((experts, tok_rows), F32)
    for choice in range(choices):
        hit = expert == ids_t[choice : choice + 1, :]
        named = named + hit.astype(F32)
        weight = weight + jnp.where(hit, gates_t[choice : choice + 1, :], 0.0)
    rank = dot(named.astype(BF16), earlier)
    owner = expert // owned
    within = expert - owner * owned
    hot = jnp.zeros((experts, tok_rows), jnp.int32)
    for host in range(owners):
        source = (host + owners // 2) % owners
        hot = jnp.where(owner == source, plan[host] - source * owned, hot)
    limit = jnp.where(within == hot, 2 * CAP, CAP)
    start = jnp.where(within == hot, 0, CAP * (1 + within + (within < hot).astype(jnp.int32)))
    rank = rank.astype(jnp.int32)
    place = jnp.where((named > 0.0) & (rank < limit), start + rank, -1)
    slot = lax.broadcasted_iota(jnp.int32, (CAP, tok_rows), 0)
    for chunk in range(owned + 1):
        picks, mixes = [], []
        for index in range(owners):
            pick = jnp.zeros((CAP, tok_rows), F32)
            mix = jnp.zeros((CAP, tok_rows), F32)
            for number in range(index * owned, (index + 1) * owned):
                match = place[number : number + 1, :] == slot + chunk * CAP
                pick = pick + match.astype(F32)
                mix = mix + jnp.where(match, weight[number : number + 1, :], 0.0)
            picks.append(pick)
            mixes.append(mix)
        pick = jnp.concatenate(picks, axis=0).astype(BF16)
        mix = jnp.concatenate(mixes, axis=0)
        outgoing[:, chunk * share : (chunk + 1) * share] = dot(pick, tokens[...]).astype(BF16)
        high = mix.astype(BF16)
        mix_high[chunk] = high
        mix_low[chunk] = (mix - high.astype(F32)).astype(BF16)


def groups_of(owned):
    return [(0, 1)] + [(number + 1,) for number in range(1, owned)]


def chunk_rows(block, chunks, share):
    return jnp.concatenate(
        [block[:, chunk * share : (chunk + 1) * share] for chunk in chunks], axis=0
    )


def projections(order, features, blocks, gate, up, group, chunks):
    share = blocks[0].shape[1] // (gate.shape[0] + 1)
    pick = order[group]
    gate_value = up_value = None
    for number, block in enumerate(blocks):
        rows = chunk_rows(block, chunks, share)
        place = pl.ds(pl.multiple_of(features[number] * share, share), share)
        gate_part = dot(rows, gate[pick, place, :])
        up_part = dot(rows, up[pick, place, :])
        gate_value = gate_part if gate_value is None else gate_value + gate_part
        up_value = up_part if up_value is None else up_value + up_part
    return gate_value, up_value


def near_kernel(count, order, features, *refs):
    blocks, (gate, up, gate_out, up_out) = refs[:count], refs[count:]
    lines = blocks[0].shape[0]
    for group, chunks in enumerate(groups_of(gate.shape[0])):
        gate_value, up_value = projections(order, features, blocks, gate, up, group, chunks)
        place = slice(chunks[0] * lines, (chunks[-1] + 1) * lines)
        gate_out[place, :] = gate_value
        up_out[place, :] = up_value


def down_parts(order, features, hidden, down, outs, lines):
    owned = down.shape[0]
    share = outs[0].shape[1] // (owned + 1)
    for number, out in enumerate(outs):
        place = pl.ds(pl.multiple_of(features[number] * share, share), share)
        for group, chunks in enumerate(groups_of(owned)):
            rows = hidden[chunks[0] * lines : (chunks[-1] + 1) * lines, :]
            value = dot(rows, down[order[group], :, place]).astype(out.dtype)
            for spot, chunk in enumerate(chunks):
                out[:, chunk * share : (chunk + 1) * share] = value[spot * lines : (spot + 1) * lines]


def far_kernel(count, order, features, *refs):
    blocks, (gate_in, up_in, gate, up, down, hidden, *outs) = refs[:count], refs[count:]
    lines = blocks[0].shape[0]
    for group, chunks in enumerate(groups_of(gate.shape[0])):
        gate_value, up_value = projections(order, features, blocks, gate, up, group, chunks)
        place = slice(chunks[0] * lines, (chunks[-1] + 1) * lines)
        gate_value = gate_value + gate_in[place, :]
        up_value = up_value + up_in[place, :]
        hidden[place, :] = (jax.nn.silu(gate_value) * up_value).astype(BF16)
    down_parts(order, features, hidden, down, outs, lines)


def own_kernel(order, features, hidden, down, *outs):
    down_parts(order, features, hidden, down, outs, outs[0].shape[0])


def mix_kernel(returned, mix_high, mix_low, out):
    chunks = mix_high.shape[0]
    share = out.shape[1]
    total = jnp.zeros(out.shape, F32)
    for chunk in range(chunks):
        rows = returned[:, chunk * share : (chunk + 1) * share]
        total = total + dot_rows(mix_high[chunk], rows) + dot_rows(mix_low[chunk], rows)
    out[...] = total.astype(out.dtype)


def call(kernel, outs, specs, *args, flops=0):
    moved = sum(a.size * a.dtype.itemsize for a in (*args, *outs))
    return pl.pallas_call(
        kernel,
        out_shape=outs,
        in_specs=specs,
        out_specs=[VMEM] * len(outs),
        compiler_params=pltpu.CompilerParams(vmem_limit_bytes=LIMIT),
        cost_estimate=pl.CostEstimate(flops=flops, bytes_accessed=moved, transcendentals=0),
    )(*args)


def swapped(value, axis, mask):
    count = lax.axis_size(axis)
    return lax.ppermute(value, axis, [(source, source ^ mask) for source in range(count)])


def per_device(tokens, expert_ids, gate_weights, replica_plan, w_gate, w_up, w_down):
    owners = lax.axis_size("expert")
    own_index = lax.axis_index("expert")
    parts = lax.axis_size("dp")
    own_part = lax.axis_index("dp")
    owned, model_width, hidden_share = w_gate.shape
    tok_rows, share = tokens.shape
    chunks = owned + 1
    lines = owners * CAP
    wide = chunks * share
    shape = jax.ShapeDtypeStruct

    outgoing, mix_high, mix_low = call(
        functools.partial(route_kernel, owned),
        [
            shape((lines, wide), BF16),
            shape((chunks, lines, tok_rows), BF16),
            shape((chunks, lines, tok_rows), BF16),
        ],
        [SMEM, VMEM, VMEM, VMEM],
        replica_plan, expert_ids, gate_weights, tokens,
    )

    def exchanged(value):
        value = value.reshape(owners, CAP, wide)
        value = lax.all_to_all(value, "expert", split_axis=0, concat_axis=0, tiled=True)
        return value.reshape(lines, wide)

    hot = replica_plan[(own_index + owners // 2) % owners] - own_index * owned
    rest = jnp.arange(owned - 1, dtype=jnp.int32)
    order = jnp.concatenate([hot[None], rest + (rest >= hot)])

    blocks = {0: exchanged(outgoing)}
    mask = parts // 2
    while mask:
        for have in list(blocks):
            blocks[have ^ mask] = swapped(blocks[have], "dp", mask)
        mask //= 2
    near = [m for m in range(parts) if m < parts // 2]
    far = [m for m in range(parts) if m >= parts // 2]
    near_features = jnp.stack([own_part ^ m for m in near]).astype(jnp.int32)
    far_features = jnp.stack([own_part ^ m for m in far]).astype(jnp.int32)
    sums = [shape((chunks * lines, hidden_share), F32)] * 2
    near_flops = 4 * len(near) * chunks * lines * share * hidden_share
    gate_sum, up_sum = call(
        functools.partial(near_kernel, len(near)),
        sums,
        [SMEM, SMEM] + [VMEM] * (len(near) + 2),
        order, near_features, *[blocks[m] for m in near], w_gate, w_up,
        flops=near_flops,
    )
    hidden, *far_outs = call(
        functools.partial(far_kernel, len(far)),
        [shape((chunks * lines, hidden_share), BF16)] + [shape((lines, wide), BF16)] * len(far),
        [SMEM, SMEM] + [VMEM] * (len(far) + 5),
        order, far_features, *[blocks[m] for m in far], gate_sum, up_sum, w_gate, w_up, w_down,
        flops=near_flops * 3 // 2,
    )

    def reduced(found):
        mask = 1
        while mask < parts // 2:
            for m in [m for m in found if m & mask]:
                arrived = swapped(found.pop(m), "dp", mask)
                found[m ^ mask] = found[m ^ mask].astype(F32) + arrived.astype(F32)
            mask *= 2
        return found

    (top, far_sum), = reduced(dict(zip(far, far_outs))).items()
    crossed = swapped(far_sum.astype(BF16), "dp", top)
    near_outs = call(
        own_kernel,
        [shape((lines, wide), BF16)] * len(near),
        [SMEM, SMEM, VMEM, VMEM],
        order, near_features, hidden, w_down,
        flops=near_flops // 2,
    )
    near_sum = reduced(dict(zip(near, near_outs)))[0]
    returned = exchanged((near_sum.astype(F32) + crossed.astype(F32)).astype(BF16))
    (mixed_out,) = call(
        mix_kernel,
        [shape((tok_rows, share), BF16)],
        [VMEM] * 3,
        returned, mix_high, mix_low,
    )
    return mixed_out


def solution(mesh):
    in_specs = (
        P("expert", "dp"),
        P("expert", None),
        P("expert", None),
        P(),
        P("expert", None, "dp"),
        P("expert", None, "dp"),
        P("expert", "dp", None),
    )
    out_specs = P("expert", "dp")
    return jax.shard_map(
        per_device, mesh=mesh, in_specs=in_specs, out_specs=out_specs, check_vma=False
    )
```

```python
import functools

import jax
import jax.numpy as jnp
from jax import lax
from jax.experimental import pallas as pl
from jax.experimental.pallas import tpu as pltpu
from jax.sharding import PartitionSpec as P

CAP = 8
F32 = jnp.float32
BF16 = jnp.bfloat16
VMEM = pl.BlockSpec(memory_space=pltpu.VMEM)
HBM = pl.BlockSpec(memory_space=pltpu.HBM)
LIMIT = 20 * 2**20


def dot(left, right):
    return jnp.dot(left, right, preferred_element_type=F32)


def dot_rows(left, right):
    return lax.dot_general(left, right, (((0,), (0,)), ((), ())), preferred_element_type=F32)


def copied(pairs, sems):
    copies = [pltpu.make_async_copy(*pair, sems.at[n]) for n, pair in enumerate(pairs)]
    for copy in copies:
        copy.start()
    return copies


def route_kernel(
    owned, plan_hbm, ids_hbm, gates_hbm, tokens_hbm, outgoing, mix_high, mix_low,
    plan, ids, gates, tokens, sems,
):
    copies = copied(
        [(plan_hbm, plan), (ids_hbm, ids), (gates_hbm, gates), (tokens_hbm, tokens)], sems
    )
    choices, tok_rows = ids.shape
    share = tokens.shape[1]
    owners = plan.shape[0]
    experts = owners * owned
    row = lax.broadcasted_iota(jnp.int32, (tok_rows, tok_rows), 0)
    col = lax.broadcasted_iota(jnp.int32, (tok_rows, tok_rows), 1)
    earlier = (row < col).astype(F32).astype(BF16)
    expert = lax.broadcasted_iota(jnp.int32, (experts, tok_rows), 0)
    owner = expert // owned
    within = expert - owner * owned
    named = jnp.zeros((experts, tok_rows), F32)
    weight = jnp.zeros((experts, tok_rows), F32)
    hot = jnp.zeros((experts, tok_rows), jnp.int32)
    copies[0].wait()
    for host in range(owners):
        source = (host + owners // 2) % owners
        hot = jnp.where(owner == source, plan[host] - source * owned, hot)
    copies[1].wait()
    copies[2].wait()
    for choice in range(choices):
        hit = expert == ids[choice : choice + 1, :]
        named = named + hit.astype(F32)
        weight = weight + jnp.where(hit, gates[choice : choice + 1, :], 0.0)
    rank = dot(named.astype(BF16), earlier)
    limit = jnp.where(within == hot, 2 * CAP, CAP)
    start = jnp.where(within == hot, 0, CAP * (1 + within + (within < hot).astype(jnp.int32)))
    rank = rank.astype(jnp.int32)
    place = jnp.where((named > 0.0) & (rank < limit), start + rank, -1)
    slot = lax.broadcasted_iota(jnp.int32, (CAP, tok_rows), 0)
    for chunk in range(owned + 1):
        picks, mixes = [], []
        for index in range(owners):
            pick = jnp.zeros((CAP, tok_rows), F32)
            mix = jnp.zeros((CAP, tok_rows), F32)
            for number in range(index * owned, (index + 1) * owned):
                match = place[number : number + 1, :] == slot + chunk * CAP
                pick = pick + match.astype(F32)
                mix = mix + jnp.where(match, weight[number : number + 1, :], 0.0)
            picks.append(pick)
            mixes.append(mix)
        pick = jnp.concatenate(picks, axis=0).astype(BF16)
        mix = jnp.concatenate(mixes, axis=0)
        if chunk == 0:
            copies[3].wait()
        outgoing[:, chunk * share : (chunk + 1) * share] = dot(pick, tokens[...]).astype(BF16)
        high = mix.astype(BF16)
        mix_high[chunk] = high
        mix_low[chunk] = (mix - high.astype(F32)).astype(BF16)


def groups_of(owned):
    return [(0, 1)] + [(number + 1,) for number in range(1, owned)]


def chunk_rows(block, chunks, share):
    return jnp.concatenate(
        [block[:, chunk * share : (chunk + 1) * share] for chunk in chunks], axis=0
    )


def projections(blocks, weights, group, chunks):
    share = blocks[0].shape[1] // (weights.shape[0] + 1)
    value = None
    for number, block in enumerate(blocks):
        rows = chunk_rows(block, chunks, share)
        part = dot(rows, weights[group, number * share : (number + 1) * share, :])
        value = part if value is None else value + part
    return value


def near_kernel(
    near, far, plan_hbm, gate_hbm, up_hbm, down_hbm, *refs
):
    blocks, refs = refs[: len(near)], refs[len(near) :]
    gate_out, up_out, gate_far, up_far, down, plan, gate, up, plan_sem, sems = refs
    owned = gate_hbm.shape[0]
    share = blocks[0].shape[1] // (owned + 1)
    lines = blocks[0].shape[0]
    owners = plan.shape[0]
    own_index, own_part = lax.axis_index("expert"), lax.axis_index("dp")
    (plan_copy,) = copied([(plan_hbm, plan)], plan_sem)
    plan_copy.wait()
    hot = plan[lax.rem(own_index + owners // 2, owners)] - own_index * owned
    order = [hot] + [n + (n >= hot).astype(jnp.int32) for n in range(owned - 1)]

    def features(m):
        return pl.ds(pl.multiple_of((own_part ^ m) * share, share), share)

    pairs = []
    for wanted, (gate_to, up_to) in ((near, (gate, up)), (far, (gate_far, up_far))):
        for group, pick in enumerate(order):
            for number, m in enumerate(wanted):
                place = slice(number * share, (number + 1) * share)
                pairs.append((gate_hbm.at[pick, features(m), :], gate_to.at[group, place, :]))
                pairs.append((up_hbm.at[pick, features(m), :], up_to.at[group, place, :]))
    for m in far + near:
        for group, pick in enumerate(order):
            place = slice(m * share, (m + 1) * share)
            pairs.append((down_hbm.at[pick, :, features(m)], down.at[group, :, place]))
    copies = copied(pairs, sems)
    for group, chunks in enumerate(groups_of(owned)):
        count = 2 * len(near)
        for copy in copies[group * count : (group + 1) * count]:
            copy.wait()
        place = slice(chunks[0] * lines, (chunks[-1] + 1) * lines)
        gate_out[place, :] = projections(blocks, gate, group, chunks)
        up_out[place, :] = projections(blocks, up, group, chunks)
    for copy in copies[2 * len(near) * owned :]:
        copy.wait()


def down_parts(numbers, hidden, down, outs, lines):
    owned = down.shape[0]
    share = outs[0].shape[1] // (owned + 1)
    for m, out in zip(numbers, outs):
        for group, chunks in enumerate(groups_of(owned)):
            rows = hidden[chunks[0] * lines : (chunks[-1] + 1) * lines, :]
            value = dot(rows, down[group, :, m * share : (m + 1) * share]).astype(out.dtype)
            for spot, chunk in enumerate(chunks):
                out[:, chunk * share : (chunk + 1) * share] = value[spot * lines : (spot + 1) * lines]


def far_kernel(far, *refs):
    blocks, (gate_in, up_in, gate, up, down, hidden, *outs) = refs[: len(far)], refs[len(far) :]
    lines = blocks[0].shape[0]
    for group, chunks in enumerate(groups_of(gate.shape[0])):
        place = slice(chunks[0] * lines, (chunks[-1] + 1) * lines)
        gate_value = projections(blocks, gate, group, chunks) + gate_in[place, :]
        up_value = projections(blocks, up, group, chunks) + up_in[place, :]
        hidden[place, :] = (jax.nn.silu(gate_value) * up_value).astype(BF16)
    down_parts(far, hidden, down, outs, lines)


def own_kernel(near, hidden, down, *outs):
    down_parts(near, hidden, down, outs, outs[0].shape[0])


def mix_kernel(returned, mix_high, mix_low, out):
    chunks = mix_high.shape[0]
    share = out.shape[1]
    total = jnp.zeros(out.shape, F32)
    for chunk in range(chunks):
        rows = returned[:, chunk * share : (chunk + 1) * share]
        total = total + dot_rows(mix_high[chunk], rows) + dot_rows(mix_low[chunk], rows)
    out[...] = total.astype(out.dtype)


def call(kernel, outs, specs, *args, scratch=(), flops=0):
    moved = sum(a.size * a.dtype.itemsize for a in (*args, *outs))
    return pl.pallas_call(
        kernel,
        out_shape=outs,
        in_specs=specs,
        out_specs=[VMEM] * len(outs),
        scratch_shapes=list(scratch),
        compiler_params=pltpu.CompilerParams(vmem_limit_bytes=LIMIT),
        cost_estimate=pl.CostEstimate(flops=flops, bytes_accessed=moved, transcendentals=0),
    )(*args)


def swapped(value, axis, mask):
    count = lax.axis_size(axis)
    return lax.ppermute(value, axis, [(source, source ^ mask) for source in range(count)])


def per_device(tokens, expert_ids, gate_weights, replica_plan, w_gate, w_up, w_down):
    owners = lax.axis_size("expert")
    parts = lax.axis_size("dp")
    owned, model_width, hidden_share = w_gate.shape
    tok_rows, share = tokens.shape
    choices = expert_ids.shape[1]
    chunks = owned + 1
    lines = owners * CAP
    wide = chunks * share
    shape = jax.ShapeDtypeStruct
    plan_memory = pltpu.SMEM((owners,), jnp.int32)

    outgoing, mix_high, mix_low = call(
        functools.partial(route_kernel, owned),
        [
            shape((lines, wide), BF16),
            shape((chunks, lines, tok_rows), BF16),
            shape((chunks, lines, tok_rows), BF16),
        ],
        [HBM] * 4,
        replica_plan, expert_ids.T, gate_weights.T, tokens,
        scratch=[
            plan_memory,
            pltpu.VMEM((choices, tok_rows), jnp.int32),
            pltpu.VMEM((choices, tok_rows), F32),
            pltpu.VMEM((tok_rows, share), BF16),
            pltpu.SemaphoreType.DMA((4,)),
        ],
    )

    def exchanged(value):
        value = value.reshape(owners, CAP, wide)
        value = lax.all_to_all(value, "expert", split_axis=0, concat_axis=0, tiled=True)
        return value.reshape(lines, wide)

    near = [m for m in range(parts) if m < parts // 2]
    far = [m for m in range(parts) if m >= parts // 2]

    def spread(blocks, mask):
        while mask:
            for have in list(blocks):
                blocks[have ^ mask] = swapped(blocks[have], "dp", mask)
            mask //= 2
        return blocks

    arrived = exchanged(outgoing)
    top = parts // 2
    crossed = swapped(arrived, "dp", top)
    blocks = spread({0: arrived}, top // 2)
    half = (owned, len(near) * share, hidden_share)
    near_flops = 4 * len(near) * chunks * lines * share * hidden_share
    halves = call(
        functools.partial(near_kernel, near, far),
        [
            shape((chunks * lines, hidden_share), F32),
            shape((chunks * lines, hidden_share), F32),
            shape(half, BF16),
            shape(half, BF16),
            shape(w_down.shape, BF16),
        ],
        [HBM] * 4 + [VMEM] * len(near),
        replica_plan, w_gate, w_up, w_down, *[blocks[m] for m in near],
        scratch=[
            plan_memory,
            pltpu.VMEM(half, BF16),
            pltpu.VMEM(half, BF16),
            pltpu.SemaphoreType.DMA((1,)),
            pltpu.SemaphoreType.DMA((6 * len(near) * owned,)),
        ],
        flops=near_flops,
    )
    crossed, *halves = lax.optimization_barrier((crossed, *halves))
    gate_sum, up_sum, gate_far, up_far, down = halves
    blocks |= spread({top: crossed}, top // 2)
    hidden, *far_outs = call(
        functools.partial(far_kernel, far),
        [shape((chunks * lines, hidden_share), BF16)] + [shape((lines, wide), BF16)] * len(far),
        [VMEM] * (len(far) + 5),
        *[blocks[m] for m in far], *halves,
        flops=near_flops * 3 // 2,
    )

    def reduced(found):
        mask = 1
        while mask < parts // 2:
            for m in [m for m in found if m & mask]:
                arrived = swapped(found.pop(m), "dp", mask)
                found[m ^ mask] = found[m ^ mask].astype(F32) + arrived.astype(F32)
            mask *= 2
        return found

    far_sum = reduced(dict(zip(far, far_outs)))[top]
    crossed = swapped(far_sum.astype(BF16), "dp", top)
    near_outs = call(
        functools.partial(own_kernel, near),
        [shape((lines, wide), BF16)] * len(near),
        [VMEM, VMEM],
        hidden, down,
        flops=near_flops // 2,
    )
    near_sum = reduced(dict(zip(near, near_outs)))[0]
    returned = exchanged((near_sum.astype(F32) + crossed.astype(F32)).astype(BF16))
    (mixed_out,) = call(
        mix_kernel,
        [shape((tok_rows, share), BF16)],
        [VMEM] * 3,
        returned, mix_high, mix_low,
    )
    return mixed_out


def solution(mesh):
    in_specs = (
        P("expert", "dp"),
        P("expert", None),
        P("expert", None),
        P(),
        P("expert", None, "dp"),
        P("expert", None, "dp"),
        P("expert", "dp", None),
    )
    out_specs = P("expert", "dp")
    return jax.shard_map(
        per_device, mesh=mesh, in_specs=in_specs, out_specs=out_specs, check_vma=False
    )
```

```python
import functools

import jax
import jax.numpy as jnp
from jax import lax
from jax.experimental import pallas as pl
from jax.experimental.pallas import tpu as pltpu
from jax.sharding import PartitionSpec as P

CAP = 8
F32 = jnp.float32
BF16 = jnp.bfloat16
VMEM = pl.BlockSpec(memory_space=pltpu.VMEM)
HBM = pl.BlockSpec(memory_space=pltpu.HBM)
LIMIT = 20 * 2**20


def dot(left, right):
    return jnp.dot(left, right, preferred_element_type=F32)


def dot_rows(left, right):
    return lax.dot_general(left, right, (((0,), (0,)), ((), ())), preferred_element_type=F32)


def copied(pairs, sems):
    copies = [pltpu.make_async_copy(*pair, sems.at[n]) for n, pair in enumerate(pairs)]
    for copy in copies:
        copy.start()
    return copies


def route_kernel(
    owned, plan_hbm, ids_hbm, gates_hbm, tokens_hbm, outgoing, mix_high, mix_low,
    plan, ids, gates, tokens, sems,
):
    copies = copied(
        [(plan_hbm, plan), (ids_hbm, ids), (gates_hbm, gates), (tokens_hbm, tokens)], sems
    )
    choices, tok_rows = ids.shape
    share = tokens.shape[1]
    owners = plan.shape[0]
    experts = owners * owned
    row = lax.broadcasted_iota(jnp.int32, (tok_rows, tok_rows), 0)
    col = lax.broadcasted_iota(jnp.int32, (tok_rows, tok_rows), 1)
    earlier = (row < col).astype(F32).astype(BF16)
    expert = lax.broadcasted_iota(jnp.int32, (experts, tok_rows), 0)
    owner = expert // owned
    within = expert - owner * owned
    named = jnp.zeros((experts, tok_rows), F32)
    weight = jnp.zeros((experts, tok_rows), F32)
    hot = jnp.zeros((experts, tok_rows), jnp.int32)
    copies[0].wait()
    for host in range(owners):
        source = (host + owners // 2) % owners
        hot = jnp.where(owner == source, plan[host] - source * owned, hot)
    copies[1].wait()
    copies[2].wait()
    for choice in range(choices):
        hit = expert == ids[choice : choice + 1, :]
        named = named + hit.astype(F32)
        weight = weight + jnp.where(hit, gates[choice : choice + 1, :], 0.0)
    rank = dot(named.astype(BF16), earlier)
    limit = jnp.where(within == hot, 2 * CAP, CAP)
    start = jnp.where(within == hot, 0, CAP * (1 + within + (within < hot).astype(jnp.int32)))
    rank = rank.astype(jnp.int32)
    place = jnp.where((named > 0.0) & (rank < limit), start + rank, -1)
    slot = lax.broadcasted_iota(jnp.int32, (CAP, tok_rows), 0)
    for chunk in range(owned + 1):
        picks, mixes = [], []
        for index in range(owners):
            pick = jnp.zeros((CAP, tok_rows), F32)
            mix = jnp.zeros((CAP, tok_rows), F32)
            for number in range(index * owned, (index + 1) * owned):
                match = place[number : number + 1, :] == slot + chunk * CAP
                pick = pick + match.astype(F32)
                mix = mix + jnp.where(match, weight[number : number + 1, :], 0.0)
            picks.append(pick)
            mixes.append(mix)
        pick = jnp.concatenate(picks, axis=0).astype(BF16)
        mix = jnp.concatenate(mixes, axis=0)
        if chunk == 0:
            copies[3].wait()
        outgoing[:, chunk * share : (chunk + 1) * share] = dot(pick, tokens[...]).astype(BF16)
        high = mix.astype(BF16)
        mix_high[chunk] = high
        mix_low[chunk] = (mix - high.astype(F32)).astype(BF16)


def groups_of(owned):
    return [(0, 1)] + [(number + 1,) for number in range(1, owned)]


def chunk_rows(block, chunks, share):
    return jnp.concatenate(
        [block[:, chunk * share : (chunk + 1) * share] for chunk in chunks], axis=0
    )


def projections(blocks, weights, group, chunks):
    share = blocks[0].shape[1] // (weights.shape[0] + 1)
    value = None
    for number, block in enumerate(blocks):
        rows = chunk_rows(block, chunks, share)
        part = dot(rows, weights[group, number * share : (number + 1) * share, :])
        value = part if value is None else value + part
    return value


def near_kernel(
    near, far, plan_hbm, gate_hbm, up_hbm, down_hbm, *refs
):
    blocks, refs = refs[: len(near)], refs[len(near) :]
    gate_out, up_out, gate_far, up_far, down, plan, gate, up, plan_sem, sems = refs
    owned = gate_hbm.shape[0]
    share = blocks[0].shape[1] // (owned + 1)
    lines = blocks[0].shape[0]
    owners = plan.shape[0]
    own_index, own_part = lax.axis_index("expert"), lax.axis_index("dp")
    (plan_copy,) = copied([(plan_hbm, plan)], plan_sem)
    plan_copy.wait()
    hot = plan[lax.rem(own_index + owners // 2, owners)] - own_index * owned
    order = [hot] + [n + (n >= hot).astype(jnp.int32) for n in range(owned - 1)]

    def features(m):
        return pl.ds(pl.multiple_of((own_part ^ m) * share, share), share)

    pairs = []
    for wanted, (gate_to, up_to) in ((near, (gate, up)), (far, (gate_far, up_far))):
        for group, pick in enumerate(order):
            for number, m in enumerate(wanted):
                place = slice(number * share, (number + 1) * share)
                pairs.append((gate_hbm.at[pick, features(m), :], gate_to.at[group, place, :]))
                pairs.append((up_hbm.at[pick, features(m), :], up_to.at[group, place, :]))
    for m in far + near:
        for group, pick in enumerate(order):
            place = slice(m * share, (m + 1) * share)
            pairs.append((down_hbm.at[pick, :, features(m)], down.at[group, :, place]))
    copies = copied(pairs, sems)
    for group, chunks in enumerate(groups_of(owned)):
        count = 2 * len(near)
        for copy in copies[group * count : (group + 1) * count]:
            copy.wait()
        place = slice(chunks[0] * lines, (chunks[-1] + 1) * lines)
        gate_out[place, :] = projections(blocks, gate, group, chunks)
        up_out[place, :] = projections(blocks, up, group, chunks)
    for copy in copies[2 * len(near) * owned :]:
        copy.wait()


def down_parts(numbers, hidden, down, outs, lines):
    owned = down.shape[0]
    share = outs[0].shape[1] // (owned + 1)
    for m, out in zip(numbers, outs):
        for group, chunks in enumerate(groups_of(owned)):
            rows = hidden[chunks[0] * lines : (chunks[-1] + 1) * lines, :]
            value = dot(rows, down[group, :, m * share : (m + 1) * share]).astype(out.dtype)
            for spot, chunk in enumerate(chunks):
                out[:, chunk * share : (chunk + 1) * share] = value[spot * lines : (spot + 1) * lines]


def far_kernel(far, *refs):
    blocks, (gate_in, up_in, gate, up, down, hidden, *outs) = refs[: len(far)], refs[len(far) :]
    lines = blocks[0].shape[0]
    for group, chunks in enumerate(groups_of(gate.shape[0])):
        place = slice(chunks[0] * lines, (chunks[-1] + 1) * lines)
        gate_value = projections(blocks, gate, group, chunks) + gate_in[place, :]
        up_value = projections(blocks, up, group, chunks) + up_in[place, :]
        hidden[place, :] = (jax.nn.silu(gate_value) * up_value).astype(BF16)
    down_parts(far, hidden, down, outs, lines)


def own_kernel(near, hidden, down, *outs):
    down_parts(near, hidden, down, outs, outs[0].shape[0])


def mix_kernel(returned, mix_high, mix_low, out):
    chunks = mix_high.shape[0]
    share = out.shape[1]
    total = jnp.zeros(out.shape, F32)
    for chunk in range(chunks):
        rows = returned[:, chunk * share : (chunk + 1) * share]
        total = total + dot_rows(mix_high[chunk], rows) + dot_rows(mix_low[chunk], rows)
    out[...] = total.astype(out.dtype)


def call(kernel, outs, specs, *args, scratch=(), flops=0):
    moved = sum(a.size * a.dtype.itemsize for a in (*args, *outs))
    return pl.pallas_call(
        kernel,
        out_shape=outs,
        in_specs=specs,
        out_specs=[VMEM] * len(outs),
        scratch_shapes=list(scratch),
        compiler_params=pltpu.CompilerParams(vmem_limit_bytes=LIMIT),
        cost_estimate=pl.CostEstimate(flops=flops, bytes_accessed=moved, transcendentals=0),
    )(*[pltpu.with_memory_space_constraint(a, s.memory_space) for a, s in zip(args, specs)])


def swapped(value, axis, mask):
    count = lax.axis_size(axis)
    return lax.ppermute(value, axis, [(source, source ^ mask) for source in range(count)])


def per_device(tokens, expert_ids, gate_weights, replica_plan, w_gate, w_up, w_down):
    owners = lax.axis_size("expert")
    parts = lax.axis_size("dp")
    owned, model_width, hidden_share = w_gate.shape
    tok_rows, share = tokens.shape
    choices = expert_ids.shape[1]
    chunks = owned + 1
    lines = owners * CAP
    wide = chunks * share
    shape = jax.ShapeDtypeStruct
    plan_memory = pltpu.SMEM((owners,), jnp.int32)

    outgoing, mix_high, mix_low = call(
        functools.partial(route_kernel, owned),
        [
            shape((lines, wide), BF16),
            shape((chunks, lines, tok_rows), BF16),
            shape((chunks, lines, tok_rows), BF16),
        ],
        [HBM] * 4,
        replica_plan, expert_ids.T, gate_weights.T, tokens,
        scratch=[
            plan_memory,
            pltpu.VMEM((choices, tok_rows), jnp.int32),
            pltpu.VMEM((choices, tok_rows), F32),
            pltpu.VMEM((tok_rows, share), BF16),
            pltpu.SemaphoreType.DMA((4,)),
        ],
    )

    def exchanged(value):
        value = value.reshape(owners, CAP, wide)
        value = lax.all_to_all(value, "expert", split_axis=0, concat_axis=0, tiled=True)
        return value.reshape(lines, wide)

    near = [m for m in range(parts) if m < parts // 2]
    far = [m for m in range(parts) if m >= parts // 2]

    def spread(blocks, mask):
        while mask:
            for have in list(blocks):
                blocks[have ^ mask] = swapped(blocks[have], "dp", mask)
            mask //= 2
        return blocks

    arrived = exchanged(outgoing)
    top = parts // 2
    crossed = swapped(arrived, "dp", top)
    blocks = spread({0: arrived}, top // 2)
    half = (owned, len(near) * share, hidden_share)
    near_flops = 4 * len(near) * chunks * lines * share * hidden_share
    halves = call(
        functools.partial(near_kernel, near, far),
        [
            shape((chunks * lines, hidden_share), F32),
            shape((chunks * lines, hidden_share), F32),
            shape(half, BF16),
            shape(half, BF16),
            shape(w_down.shape, BF16),
        ],
        [HBM] * 4 + [VMEM] * len(near),
        replica_plan, w_gate, w_up, w_down, *[blocks[m] for m in near],
        scratch=[
            plan_memory,
            pltpu.VMEM(half, BF16),
            pltpu.VMEM(half, BF16),
            pltpu.SemaphoreType.DMA((1,)),
            pltpu.SemaphoreType.DMA((6 * len(near) * owned,)),
        ],
        flops=near_flops,
    )
    crossed, *halves = lax.optimization_barrier((crossed, *halves))
    gate_sum, up_sum, gate_far, up_far, down = halves
    blocks |= spread({top: crossed}, top // 2)
    hidden, *far_outs = call(
        functools.partial(far_kernel, far),
        [shape((chunks * lines, hidden_share), BF16)] + [shape((lines, wide), BF16)] * len(far),
        [VMEM] * (len(far) + 5),
        *[blocks[m] for m in far], *halves,
        flops=near_flops * 3 // 2,
    )

    def reduced(found):
        mask = 1
        while mask < parts // 2:
            for m in [m for m in found if m & mask]:
                arrived = swapped(found.pop(m), "dp", mask)
                found[m ^ mask] = found[m ^ mask].astype(F32) + arrived.astype(F32)
            mask *= 2
        return found

    far_sum = reduced(dict(zip(far, far_outs)))[top]
    crossed = swapped(far_sum.astype(BF16), "dp", top)
    near_outs = call(
        functools.partial(own_kernel, near),
        [shape((lines, wide), BF16)] * len(near),
        [VMEM, VMEM],
        hidden, down,
        flops=near_flops // 2,
    )
    near_sum = reduced(dict(zip(near, near_outs)))[0]
    returned = exchanged((near_sum.astype(F32) + crossed.astype(F32)).astype(BF16))
    (mixed_out,) = call(
        mix_kernel,
        [shape((tok_rows, share), BF16)],
        [VMEM] * 3,
        returned, mix_high, mix_low,
    )
    return mixed_out


def solution(mesh):
    in_specs = (
        P("expert", "dp"),
        P("expert", None),
        P("expert", None),
        P(),
        P("expert", None, "dp"),
        P("expert", None, "dp"),
        P("expert", "dp", None),
    )
    out_specs = P("expert", "dp")
    return jax.shard_map(
        per_device, mesh=mesh, in_specs=in_specs, out_specs=out_specs, check_vma=False
    )
```

```python
import functools

import jax
import jax.numpy as jnp
from jax import lax
from jax.experimental import pallas as pl
from jax.experimental.pallas import tpu as pltpu
from jax.sharding import PartitionSpec as P

CAP = 8
F32 = jnp.float32
BF16 = jnp.bfloat16
HBM = pl.BlockSpec(memory_space=pltpu.HBM)
VMEM = pl.BlockSpec(memory_space=pltpu.VMEM)
LIMIT = 20 * 2**20


def dot(left, right):
    return jnp.dot(left, right, preferred_element_type=F32)


def dot_rows(left, right):
    return lax.dot_general(left, right, (((0,), (0,)), ((), ())), preferred_element_type=F32)


def route_kernel(owned, low, plan_hbm, ids_hbm, gates_hbm, tokens_hbm, *refs):
    lots, (info, mix_high, mix_low) = refs[:low], refs[low : low + 3]
    plan, ids, gates, tokens, place, weight, sems = refs[low + 3 :]
    sources = (plan_hbm, ids_hbm, gates_hbm, tokens_hbm)
    copies = [
        pltpu.make_async_copy(source, target, sems.at[n])
        for n, (source, target) in enumerate(zip(sources, (plan, ids, gates, tokens)))
    ]
    for copy in copies:
        copy.start()
    choices, tok_rows = ids.shape
    share = tokens.shape[1]
    owners = plan.shape[0]
    high = owners // low
    experts = owners * owned
    own_index = lax.axis_index("expert")
    row = lax.broadcasted_iota(jnp.int32, (tok_rows, tok_rows), 0)
    col = lax.broadcasted_iota(jnp.int32, (tok_rows, tok_rows), 1)
    earlier = (row < col).astype(F32).astype(BF16)
    expert = lax.broadcasted_iota(jnp.int32, (experts, tok_rows), 0)
    owner = expert // owned
    within = expert - owner * owned
    named = jnp.zeros((experts, tok_rows), F32)
    weights = jnp.zeros((experts, tok_rows), F32)
    hot = jnp.zeros((experts, tok_rows), jnp.int32)
    copies[0].wait()
    for host in range(owners):
        source = (host + owners // 2) % owners
        hot = jnp.where(owner == source, plan[host] - source * owned, hot)
    own_hot = plan[lax.rem(own_index + owners // 2, owners)] - own_index * owned
    info[...] = jnp.full(info.shape, own_hot, jnp.int32)
    copies[1].wait()
    copies[2].wait()
    for choice in range(choices):
        hit = expert == ids[choice : choice + 1, :]
        named = named + hit.astype(F32)
        weights = weights + jnp.where(hit, gates[choice : choice + 1, :], 0.0)
    weight[...] = weights
    rank = dot(named.astype(BF16), earlier).astype(jnp.int32)
    limit = jnp.where(within == hot, 2 * CAP, CAP)
    start = jnp.where(within == hot, 0, CAP * (1 + within + (within < hot).astype(jnp.int32)))
    place[...] = jnp.where((named > 0.0) & (rank < limit), start + rank, -1)
    slot = lax.broadcasted_iota(jnp.int32, (CAP, tok_rows), 0)
    zero = jnp.zeros((CAP, tok_rows), F32)
    copies[3].wait()
    for chunk in range(owned + 1):
        picks, mixes = [], []
        for m in range(low):
            for k in range(high):
                index = own_index ^ (k * low + m)
                pick, mix = zero, zero
                for number in range(owned):
                    line = pl.ds(index * owned + number, 1)
                    match = place[line, :] == slot + chunk * CAP
                    pick = pick + match.astype(F32)
                    mix = mix + jnp.where(match, weight[line, :], 0.0)
                picks.append(pick)
                mixes.append(mix)
        pick = jnp.concatenate(picks, axis=0).astype(BF16)
        values = dot(pick, tokens[...]).astype(BF16)
        for m, lot in enumerate(lots):
            lines = slice(m * high * CAP, (m + 1) * high * CAP)
            lot[:, chunk * share : (chunk + 1) * share] = values[lines]
        straight = [mixes[k] if m == 0 else zero for k in range(high) for m in range(low)]
        mix = jnp.concatenate(straight + mixes[high:], axis=0)
        rounded = mix.astype(BF16)
        mix_high[chunk] = rounded
        mix_low[chunk] = (mix - rounded.astype(F32)).astype(BF16)


def join_kernel(low, *refs):
    lots, pieces = refs[:low], refs[low:]
    values = [lot[...].astype(F32) for lot in lots]
    for k, piece in enumerate(pieces):
        rows = [value[k * CAP : (k + 1) * CAP] for value in values]
        piece[...] = jnp.concatenate(rows, axis=0).astype(BF16)


def split_kernel(high, *refs):
    pieces, lots = refs[:high], refs[high:]
    values = [piece[...].astype(F32) for piece in pieces]
    for m, lot in enumerate(lots):
        rows = [value[(m + 1) * CAP : (m + 2) * CAP] for value in values]
        lot[...] = jnp.concatenate(rows, axis=0).astype(BF16)


def groups_of(owned):
    return [(0, 1)] + [(number + 1,) for number in range(1, owned)]


def order_of(info, owned):
    hot = jnp.max(info[...].astype(F32)).astype(jnp.int32)
    return [hot] + [n + (n >= hot).astype(jnp.int32) for n in range(owned - 1)]


def features_of(m, share):
    return pl.ds(pl.multiple_of((lax.axis_index("dp") ^ m) * share, share), share)


def projections(order, numbers, blocks, gate, up):
    owned = gate.shape[0]
    share = blocks[0][0].shape[1] // (owned + 1)
    for group, chunks in enumerate(groups_of(owned)):
        gate_value = up_value = None
        for m, pieces in zip(numbers, blocks):
            rows = jnp.concatenate(
                [p[:, c * share : (c + 1) * share] for c in chunks for p in pieces], axis=0
            )
            gate_part = dot(rows, gate[order[group], features_of(m, share), :])
            up_part = dot(rows, up[order[group], features_of(m, share), :])
            gate_value = gate_part if gate_value is None else gate_value + gate_part
            up_value = up_part if up_value is None else up_value + up_part
        yield chunks, gate_value, up_value


def listed(refs, count, size):
    return [refs[n * size : (n + 1) * size] for n in range(count)], refs[count * size :]


def near_kernel(near, high, info, gate, up, *refs):
    blocks, (gate_out, up_out) = listed(refs, len(near), high)
    lines = high * blocks[0][0].shape[0]
    order = order_of(info, gate.shape[0])
    for chunks, gate_value, up_value in projections(order, near, blocks, gate, up):
        place = slice(chunks[0] * lines, (chunks[-1] + 1) * lines)
        gate_out[place, :] = gate_value
        up_out[place, :] = up_value


def down_parts(order, numbers, hidden, down, outs):
    owned = down.shape[0]
    lines, wide = outs[0].shape
    share = wide // (owned + 1)
    for m, out in zip(numbers, outs):
        for group, chunks in enumerate(groups_of(owned)):
            rows = hidden[chunks[0] * lines : (chunks[-1] + 1) * lines, :]
            value = dot(rows, down[order[group], :, features_of(m, share)]).astype(out.dtype)
            for spot, chunk in enumerate(chunks):
                out[:, chunk * share : (chunk + 1) * share] = value[spot * lines : (spot + 1) * lines]


def far_kernel(far, high, info, gate, up, down, gate_in, up_in, *refs):
    blocks, (hidden, *outs) = listed(refs, len(far), high)
    lines = outs[0].shape[0]
    order = order_of(info, gate.shape[0])
    for chunks, gate_value, up_value in projections(order, far, blocks, gate, up):
        place = slice(chunks[0] * lines, (chunks[-1] + 1) * lines)
        gate_value = gate_value + gate_in[place, :]
        up_value = up_value + up_in[place, :]
        hidden[place, :] = (jax.nn.silu(gate_value) * up_value).astype(BF16)
    down_parts(order, far, hidden, down, outs)


def own_kernel(near, info, down, hidden, *outs):
    down_parts(order_of(info, down.shape[0]), near, hidden, down, outs)


def sum_kernel(count, *refs):
    terms, pieces = refs[:count], refs[count:]
    size = pieces[0].shape[0]
    for k, piece in enumerate(pieces):
        total = sum(term[k * size : (k + 1) * size, :].astype(F32) for term in terms)
        piece[...] = total.astype(piece.dtype)


def mix_kernel(count, mix_high, mix_low, *refs):
    arrays, out = refs[:count], refs[count]
    share = out.shape[1]
    total = jnp.zeros(out.shape, F32)
    for chunk in range(mix_high.shape[0]):
        rows = jnp.concatenate([a[:, chunk * share : (chunk + 1) * share] for a in arrays], axis=0)
        total = total + dot_rows(mix_high[chunk], rows) + dot_rows(mix_low[chunk], rows)
    out[...] = total.astype(out.dtype)


def call(kernel, outs, *args, specs=None, scratch=(), flops=0):
    moved = sum(a.size * a.dtype.itemsize for a in (*args, *outs))
    if specs:
        args = [
            pltpu.with_memory_space_constraint(a, s.memory_space) for a, s in zip(args, specs)
        ]
    return pl.pallas_call(
        kernel,
        out_shape=outs,
        in_specs=specs or [VMEM] * len(args),
        out_specs=[VMEM] * len(outs),
        scratch_shapes=list(scratch),
        compiler_params=pltpu.CompilerParams(vmem_limit_bytes=LIMIT),
        cost_estimate=pl.CostEstimate(flops=flops, bytes_accessed=moved, transcendentals=0),
    )(*args)


def swapped(value, axis, mask):
    count = lax.axis_size(axis)
    return lax.ppermute(value, axis, [(source, source ^ mask) for source in range(count)])


def per_device(tokens, expert_ids, gate_weights, replica_plan, w_gate, w_up, w_down):
    owners = lax.axis_size("expert")
    parts = lax.axis_size("dp")
    owned, model_width, hidden_share = w_gate.shape
    tok_rows, share = tokens.shape
    choices = expert_ids.shape[1]
    chunks = owned + 1
    lines = owners * CAP
    wide = chunks * share
    low = 1 << ((owners.bit_length() - 1) // 2)
    high = owners // low
    shape = jax.ShapeDtypeStruct
    lot = shape((high * CAP, wide), BF16)
    piece = shape((low * CAP, wide), BF16)
    whole = shape((lines, wide), BF16)
    mixes = shape((chunks, lines + (low - 1) * high * CAP, tok_rows), BF16)

    *lots, info, mix_high, mix_low = call(
        functools.partial(route_kernel, owned, low),
        [lot] * low + [shape((8, 128), jnp.int32), mixes, mixes],
        replica_plan, expert_ids.T, gate_weights.T, tokens,
        specs=[HBM] * 4,
        scratch=[
            pltpu.SMEM((owners,), jnp.int32),
            pltpu.VMEM((choices, tok_rows), jnp.int32),
            pltpu.VMEM((choices, tok_rows), F32),
            pltpu.VMEM((tok_rows, share), BF16),
            pltpu.VMEM((owners * owned, tok_rows), jnp.int32),
            pltpu.VMEM((owners * owned, tok_rows), F32),
            pltpu.SemaphoreType.DMA((4,)),
        ],
        flops=4 * 10**10,
    )
    lots = [lots[0]] + [swapped(lots[m], "expert", m) for m in range(1, low)]
    pieces = call(functools.partial(join_kernel, low), [piece] * high, *lots)
    arrived = {k: swapped(pieces[k], "expert", k * low) for k in range(high - 1, 0, -1)}
    arrived[0] = pieces[0]

    near = [m for m in range(parts) if m < parts // 2]
    far = [m for m in range(parts) if m >= parts // 2]
    top = parts // 2
    blocks = {m: {} for m in range(parts)}
    for k in range(high):
        blocks[0][k] = arrived[k]
        blocks[top][k] = swapped(arrived[k], "dp", top)
        mask = top // 2
        while mask:
            for m in range(0, parts, 2 * mask):
                blocks[m ^ mask][k] = swapped(blocks[m][k], "dp", mask)
            mask //= 2

    def flat(numbers):
        return [blocks[m][k] for m in numbers for k in range(high)]

    near_flops = 4 * len(near) * chunks * lines * share * hidden_share
    sums = [shape((chunks * lines, hidden_share), F32)] * 2
    gate_sum, up_sum = call(
        functools.partial(near_kernel, near, high),
        sums,
        info, w_gate, w_up, *flat(near),
        flops=near_flops,
    )
    hidden, *far_outs = call(
        functools.partial(far_kernel, far, high),
        [shape((chunks * lines, hidden_share), BF16)] + [whole] * len(far),
        info, w_gate, w_up, w_down, gate_sum, up_sum, *flat(far),
        flops=near_flops * 3 // 2,
    )

    def reduced(found):
        mask = 1
        while 2 * mask < top:
            for m in [m for m in found if m & mask]:
                there = swapped(found.pop(m), "dp", mask)
                (found[m ^ mask],) = call(
                    functools.partial(sum_kernel, 2), [whole], found[m ^ mask], there
                )
            mask *= 2
        terms = []
        for m, value in found.items():
            terms.append(swapped(value, "dp", mask) if m & mask else value)
        return call(functools.partial(sum_kernel, len(terms)), [piece] * high, *terms)

    far_pieces = reduced(dict(zip(far, far_outs)))
    crossed = {k: swapped(far_pieces[k], "dp", top) for k in range(high - 1, -1, -1)}
    near_outs = call(
        functools.partial(own_kernel, near),
        [whole] * len(near),
        info, w_down, hidden,
        flops=near_flops // 2,
    )
    near_pieces = reduced(dict(zip(near, near_outs)))
    back = {}
    for k in range(high - 1, -1, -1):
        (total,) = call(functools.partial(sum_kernel, 2), [piece], near_pieces[k], crossed[k])
        back[k] = swapped(total, "expert", k * low) if k else total
    back = [back[k] for k in range(high)]
    others = call(functools.partial(split_kernel, high), [lot] * (low - 1), *back)
    others = [swapped(others[m - 1], "expert", m) for m in range(1, low)]
    (mixed_out,) = call(
        functools.partial(mix_kernel, high + low - 1),
        [shape((tok_rows, share), BF16)],
        mix_high, mix_low, *back, *others,
    )
    return mixed_out


def solution(mesh):
    in_specs = (
        P("expert", "dp"),
        P("expert", None),
        P("expert", None),
        P(),
        P("expert", None, "dp"),
        P("expert", None, "dp"),
        P("expert", "dp", None),
    )
    out_specs = P("expert", "dp")
    return jax.shard_map(
        per_device, mesh=mesh, in_specs=in_specs, out_specs=out_specs, check_vma=False
    )
```

```python
import functools

import jax
import jax.numpy as jnp
from jax import lax
from jax.experimental import pallas as pl
from jax.experimental.pallas import tpu as pltpu
from jax.sharding import PartitionSpec as P

CAP = 8
F32 = jnp.float32
BF16 = jnp.bfloat16
HBM = pl.BlockSpec(memory_space=pltpu.HBM)
VMEM = pl.BlockSpec(memory_space=pltpu.VMEM)
LIMIT = 20 * 2**20


def dot(left, right):
    return jnp.dot(left, right, preferred_element_type=F32)


def dot_rows(left, right):
    return lax.dot_general(left, right, (((0,), (0,)), ((), ())), preferred_element_type=F32)


def route_kernel(owned, low, high_steps, plan_hbm, ids_hbm, gates_hbm, tokens_hbm, *refs):
    high = len(high_steps)
    pieces, (info, mixtures, plan, ids, gates, tokens, place, weight, sems) = refs[:high], refs[high:]
    sources = (plan_hbm, ids_hbm, gates_hbm, tokens_hbm)
    copies = [
        pltpu.make_async_copy(source, target, sems.at[n])
        for n, (source, target) in enumerate(zip(sources, (plan, ids, gates, tokens)))
    ]
    for copy in copies:
        copy.start()
    choices, tok_rows = ids.shape
    share = tokens.shape[1]
    owners = plan.shape[0]
    experts = owners * owned
    steps = [(k, m) for k in high_steps for m in range(low)]
    own_index = lax.axis_index("expert")
    row = lax.broadcasted_iota(jnp.int32, (tok_rows, tok_rows), 0)
    col = lax.broadcasted_iota(jnp.int32, (tok_rows, tok_rows), 1)
    earlier = (row < col).astype(F32).astype(BF16)
    expert = lax.broadcasted_iota(jnp.int32, (experts, tok_rows), 0)
    owner = expert // owned
    within = expert - owner * owned
    named = jnp.zeros((experts, tok_rows), F32)
    weights = jnp.zeros((experts, tok_rows), F32)
    hot = jnp.zeros((experts, tok_rows), jnp.int32)
    copies[0].wait()
    for host in range(owners):
        source = (host + owners // 2) % owners
        hot = jnp.where(owner == source, plan[host] - source * owned, hot)
    own_hot = plan[lax.rem(own_index + owners // 2, owners)] - own_index * owned
    info[...] = jnp.full(info.shape, own_hot, jnp.int32)
    copies[1].wait()
    copies[2].wait()
    for choice in range(choices):
        hit = expert == ids[choice : choice + 1, :]
        named = named + hit.astype(F32)
        weights = weights + jnp.where(hit, gates[choice : choice + 1, :], 0.0)
    weight[...] = weights
    rank = dot(named.astype(BF16), earlier).astype(jnp.int32)
    limit = jnp.where(within == hot, 2 * CAP, CAP)
    start = jnp.where(within == hot, 0, CAP * (1 + within + (within < hot).astype(jnp.int32)))
    place[...] = jnp.where((named > 0.0) & (rank < limit), start + rank, -1)
    slot = lax.broadcasted_iota(jnp.int32, (CAP, tok_rows), 0)
    zero = jnp.zeros((CAP, tok_rows), F32)
    copies[3].wait()
    for chunk in range(owned + 1):
        picks, mixes = [], []
        for k, m in steps:
            index = own_index ^ (k * low + m)
            pick, mix = zero, zero
            for number in range(owned):
                line = pl.ds(index * owned + number, 1)
                match = place[line, :] == slot + chunk * CAP
                pick = pick + match.astype(F32)
                mix = mix + jnp.where(match, weight[line, :], 0.0)
            picks.append(pick)
            mixes.append(mix)
        pick = jnp.concatenate(picks, axis=0).astype(BF16)
        values = dot(pick, tokens[...]).astype(BF16)
        size = low * CAP
        for n, piece in enumerate(pieces):
            piece[:, chunk * share : (chunk + 1) * share] = values[n * size : (n + 1) * size]
        mix = jnp.concatenate(mixes, axis=0)
        rounded = mix.astype(BF16)
        mixtures[chunk, 0] = rounded
        mixtures[chunk, 1] = (mix - rounded.astype(F32)).astype(BF16)


def blocks_of(value):
    return [value[begin : begin + CAP] for begin in range(0, value.shape[0], CAP)]


def regroup_kernel(count, moves, *refs):
    values = [blocks_of(ref[...].astype(F32)) for ref in refs[:count]]
    for out, blocks in zip(refs[count:], moves):
        out[...] = jnp.concatenate([values[n][b] for n, b in blocks], axis=0).astype(out.dtype)


def sum_kernel(count, moves, *refs):
    values = [blocks_of(ref[...].astype(F32)) for ref in refs[:count]]
    for out, blocks in zip(refs[count:], moves):
        rows = [sum(values[n][b] for n, b in terms) for terms in blocks]
        out[...] = jnp.concatenate(rows, axis=0).astype(out.dtype)


def groups_of(owned):
    return [(0, 1)] + [(number + 1,) for number in range(1, owned)]


def order_of(info, owned):
    hot = jnp.max(info[...].astype(F32)).astype(jnp.int32)
    return [hot] + [n + (n >= hot).astype(jnp.int32) for n in range(owned - 1)]


def features_of(m, share):
    return pl.ds(pl.multiple_of((lax.axis_index("dp") ^ m) * share, share), share)


def projections(order, numbers, blocks, gate, up):
    owned = gate.shape[0]
    share = blocks[0].shape[1] // (owned + 1)
    for group, chunks in enumerate(groups_of(owned)):
        gate_value = up_value = None
        for m, block in zip(numbers, blocks):
            rows = jnp.concatenate([block[:, c * share : (c + 1) * share] for c in chunks], axis=0)
            gate_part = dot(rows, gate[order[group], features_of(m, share), :])
            up_part = dot(rows, up[order[group], features_of(m, share), :])
            gate_value = gate_part if gate_value is None else gate_value + gate_part
            up_value = up_part if up_value is None else up_value + up_part
        lines = block.shape[0]
        yield slice(chunks[0] * lines, (chunks[-1] + 1) * lines), gate_value, up_value


def first_kernel(numbers, info, gate, up, down, *refs):
    *blocks, gate_out, up_out = refs
    order = order_of(info, gate.shape[0])
    for place, gate_value, up_value in projections(order, numbers, blocks, gate, up):
        gate_out[place, :] = gate_value
        up_out[place, :] = up_value


def down_parts(order, numbers, hidden, down, outs):
    owned = down.shape[0]
    lines, wide = outs[0].shape
    share = wide // (owned + 1)
    for m, out in zip(numbers, outs):
        for group, chunks in enumerate(groups_of(owned)):
            rows = hidden[chunks[0] * lines : (chunks[-1] + 1) * lines, :]
            value = dot(rows, down[order[group], :, features_of(m, share)]).astype(out.dtype)
            for spot, chunk in enumerate(chunks):
                out[:, chunk * share : (chunk + 1) * share] = value[spot * lines : (spot + 1) * lines]


def second_kernel(numbers, out_number, info, gate, up, down, gate_in, up_in, *refs):
    *blocks, hidden, out = refs
    order = order_of(info, gate.shape[0])
    for place, gate_value, up_value in projections(order, numbers, blocks, gate, up):
        gate_value = gate_value + gate_in[place, :]
        up_value = up_value + up_in[place, :]
        hidden[place, :] = (jax.nn.silu(gate_value) * up_value).astype(BF16)
    down_parts(order, [out_number], hidden, down, [out])


def down_kernel(numbers, info, down, hidden, *outs):
    down_parts(order_of(info, down.shape[0]), numbers, hidden, down, outs)


def mix_kernel(mixtures, *refs):
    *pieces, out = refs
    share = out.shape[1]
    total = jnp.zeros(out.shape, F32)
    for chunk in range(mixtures.shape[0]):
        rows = jnp.concatenate([p[:, chunk * share : (chunk + 1) * share] for p in pieces], axis=0)
        total = total + dot_rows(mixtures[chunk, 0], rows) + dot_rows(mixtures[chunk, 1], rows)
    out[...] = total.astype(out.dtype)


def call(kernel, outs, *args, specs=None, scratch=(), flops=0):
    if specs:
        args = [
            pltpu.with_memory_space_constraint(a, s.memory_space) for a, s in zip(args, specs)
        ]
    return pl.pallas_call(
        kernel,
        out_shape=outs,
        in_specs=specs or [VMEM] * len(args),
        out_specs=[VMEM] * len(outs),
        scratch_shapes=list(scratch),
        compiler_params=pltpu.CompilerParams(vmem_limit_bytes=LIMIT),
        cost_estimate=pl.CostEstimate(flops=flops + 1000, bytes_accessed=1000, transcendentals=0),
    )(*args)


def swapped(value, axis, mask):
    count = lax.axis_size(axis)
    return lax.ppermute(value, axis, [(source, source ^ mask) for source in range(count)])


def turned(value, low_step, across):
    parts = lax.axis_size("dp")
    if not across:
        return swapped(value, "expert", low_step)
    return swapped(value, ("expert", "dp"), low_step * parts + across)


def per_device(tokens, expert_ids, gate_weights, replica_plan, w_gate, w_up, w_down):
    owners = lax.axis_size("expert")
    parts = lax.axis_size("dp")
    owned, model_width, hidden_share = w_gate.shape
    tok_rows, share = tokens.shape
    choices = expert_ids.shape[1]
    chunks = owned + 1
    lines = owners * CAP
    wide = chunks * share
    low = 1 << ((owners.bit_length() - 1) // 2)
    high = owners // low
    high_steps = list(range(high - 1, -1, -1))
    ways_in = [high_steps]
    ways_out = [high_steps[: high // 2], high_steps[high // 2 :]]
    shape = jax.ShapeDtypeStruct
    piece = shape((low * CAP, wide), BF16)
    whole = shape((lines, wide), BF16)

    def lot(group):
        return shape((len(group) * CAP, wide), BF16)

    *pieces, info, mixtures = call(
        functools.partial(route_kernel, owned, low, high_steps),
        [piece] * high
        + [shape((8, 128), jnp.int32), shape((chunks, 2, lines, tok_rows), BF16)],
        replica_plan, expert_ids.T, gate_weights.T, tokens,
        specs=[HBM] * 4,
        scratch=[
            pltpu.SMEM((owners,), jnp.int32),
            pltpu.VMEM((choices, tok_rows), jnp.int32),
            pltpu.VMEM((choices, tok_rows), F32),
            pltpu.VMEM((tok_rows, share), BF16),
            pltpu.VMEM((owners * owned, tok_rows), jnp.int32),
            pltpu.VMEM((owners * owned, tok_rows), F32),
            pltpu.SemaphoreType.DMA((4,)),
        ],
        flops=16 * 10**10,
    )
    arrived = {k: swapped(p, "expert", k * low) if k else p for k, p in zip(high_steps, pieces)}

    top = parts // 2
    rows, here, there = [], [], []
    for group in ways_in:
        lots = call(
            functools.partial(regroup_kernel, len(group), [
                [(n, m) for n in range(len(group))] for m in range(low)
            ]),
            [lot(group)] * low,
            *[arrived[k] for k in group],
        )
        there += [turned(value, m, top) for m, value in enumerate(lots)]
        here += [turned(value, m, 0) if m else value for m, value in enumerate(lots)]
        rows += [(k, m) for m in range(low) for k in group]
    moves = [(n, b) for n, value in enumerate(here) for b in range(value.shape[0] // CAP)]
    moves = [moves, [(n + len(here), b) for n, b in moves]]
    here, there = call(
        functools.partial(regroup_kernel, 2 * len(here), moves), [whole] * 2, *here, *there
    )
    blocks = {0: here, top: there}
    mask = top // 2
    while mask:
        for n in list(blocks):
            blocks[n ^ mask] = swapped(blocks[n], "dp", mask)
        mask //= 2
    first = [0, top]
    second = [n for n in range(parts) if n not in first]
    sums = [shape((chunks * lines, hidden_share), F32)] * 2
    gate_sum, up_sum = call(
        functools.partial(first_kernel, first),
        sums,
        info, w_gate, w_up, w_down, *[blocks[n] for n in first],
    )
    outs = {}
    hidden, outs[parts - 1] = call(
        functools.partial(second_kernel, second, parts - 1),
        [shape((chunks * lines, hidden_share), BF16), whole],
        info, w_gate, w_up, w_down, gate_sum, up_sum, *[blocks[n] for n in second],
    )
    far, near = list(range(top, parts - 1)), list(range(top))
    for numbers in (far, near):
        found = call(
            functools.partial(down_kernel, numbers), [whole] * len(numbers), info, w_down, hidden
        )
        outs |= dict(zip(numbers, found))

    def reduced(begin):
        found = {n: outs[n] for n in range(begin, begin + top)}
        mask = 1
        while 2 * mask < top:
            for n in [n for n in found if n & mask]:
                value = swapped(found.pop(n), "dp", mask)
                (found[n ^ mask],) = call(
                    functools.partial(sum_kernel, 2, [
                        [[(0, b), (1, b)] for b in range(len(rows))]
                    ]),
                    [whole], found[n ^ mask], value,
                )
            mask *= 2
        terms = [swapped(value, "dp", mask) if n & mask else value for n, value in found.items()]
        moves = [
            [[(t, rows.index((k, m))) for t in range(len(terms))] for k in group]
            for group in ways_out for m in range(low)
        ]
        sums = call(
            functools.partial(sum_kernel, len(terms), moves),
            [lot(group) for group in ways_out for m in range(low)],
            *terms,
        )
        return [sums[n : n + low] for n in range(0, len(sums), low)]

    back = {}
    for group, far_lots, near_lots in zip(ways_out, reduced(top), reduced(0)):
        terms = []
        for m in range(low):
            terms.append(turned(far_lots[m], m, top))
            terms.append(turned(near_lots[m], m, 0) if m else near_lots[m])
        moves = [[[(2 * m, n), (2 * m + 1, n)] for m in range(low)] for n in range(len(group))]
        totals = call(
            functools.partial(sum_kernel, 2 * low, moves), [piece] * len(group), *terms
        )
        for k, value in zip(group, totals):
            back[k] = swapped(value, "expert", k * low) if k else value
    (mixed_out,) = call(
        mix_kernel,
        [shape((tok_rows, share), BF16)],
        mixtures, *[back[k] for k in high_steps],
    )
    return mixed_out


def solution(mesh):
    in_specs = (
        P("expert", "dp"),
        P("expert", None),
        P("expert", None),
        P(),
        P("expert", None, "dp"),
        P("expert", None, "dp"),
        P("expert", "dp", None),
    )
    out_specs = P("expert", "dp")
    return jax.shard_map(
        per_device, mesh=mesh, in_specs=in_specs, out_specs=out_specs, check_vma=False
    )
```

```python
import functools

import jax
import jax.numpy as jnp
from jax import lax
from jax.experimental import pallas as pl
from jax.experimental.pallas import tpu as pltpu
from jax.sharding import PartitionSpec as P

CAP = 8
F32 = jnp.float32
BF16 = jnp.bfloat16
HBM = pl.BlockSpec(memory_space=pltpu.HBM)
VMEM = pl.BlockSpec(memory_space=pltpu.VMEM)
LIMIT = 20 * 2**20


def dot(left, right):
    return jnp.dot(left, right, preferred_element_type=F32)


def dot_rows(left, right):
    return lax.dot_general(left, right, (((0,), (0,)), ((), ())), preferred_element_type=F32)


def route_kernel(owned, low, high_steps, plan_hbm, ids_hbm, gates_hbm, tokens_hbm, *refs):
    high = len(high_steps)
    pieces, (info, mixtures, plan, ids, gates, tokens, place, weight, sems) = refs[:high], refs[high:]
    sources = (plan_hbm, ids_hbm, gates_hbm, tokens_hbm)
    copies = [
        pltpu.make_async_copy(source, target, sems.at[n])
        for n, (source, target) in enumerate(zip(sources, (plan, ids, gates, tokens)))
    ]
    for copy in copies:
        copy.start()
    choices, tok_rows = ids.shape
    share = tokens.shape[1]
    owners = plan.shape[0]
    experts = owners * owned
    steps = [(k, m) for k in high_steps for m in range(low)]
    own_index = lax.axis_index("expert")
    row = lax.broadcasted_iota(jnp.int32, (tok_rows, tok_rows), 0)
    col = lax.broadcasted_iota(jnp.int32, (tok_rows, tok_rows), 1)
    earlier = (row < col).astype(F32).astype(BF16)
    expert = lax.broadcasted_iota(jnp.int32, (experts, tok_rows), 0)
    owner = expert // owned
    within = expert - owner * owned
    named = jnp.zeros((experts, tok_rows), F32)
    weights = jnp.zeros((experts, tok_rows), F32)
    hot = jnp.zeros((experts, tok_rows), jnp.int32)
    copies[0].wait()
    for host in range(owners):
        source = (host + owners // 2) % owners
        hot = jnp.where(owner == source, plan[host] - source * owned, hot)
    own_hot = plan[lax.rem(own_index + owners // 2, owners)] - own_index * owned
    info[...] = jnp.full(info.shape, own_hot, jnp.int32)
    copies[1].wait()
    copies[2].wait()
    for choice in range(choices):
        hit = expert == ids[choice : choice + 1, :]
        named = named + hit.astype(F32)
        weights = weights + jnp.where(hit, gates[choice : choice + 1, :], 0.0)
    weight[...] = weights
    rank = dot(named.astype(BF16), earlier).astype(jnp.int32)
    limit = jnp.where(within == hot, 2 * CAP, CAP)
    start = jnp.where(within == hot, 0, CAP * (1 + within + (within < hot).astype(jnp.int32)))
    place[...] = jnp.where((named > 0.0) & (rank < limit), start + rank, -1)
    slot = lax.broadcasted_iota(jnp.int32, (CAP, tok_rows), 0)
    zero = jnp.zeros((CAP, tok_rows), F32)
    copies[3].wait()
    for chunk in range(owned + 1):
        picks, mixes = [], []
        for k, m in steps:
            index = own_index ^ (k * low + m)
            pick, mix = zero, zero
            for number in range(owned):
                line = pl.ds(index * owned + number, 1)
                match = place[line, :] == slot + chunk * CAP
                pick = pick + match.astype(F32)
                mix = mix + jnp.where(match, weight[line, :], 0.0)
            picks.append(pick)
            mixes.append(mix)
        pick = jnp.concatenate(picks, axis=0).astype(BF16)
        values = dot(pick, tokens[...]).astype(BF16)
        size = low * CAP
        for n, piece in enumerate(pieces):
            piece[:, chunk * share : (chunk + 1) * share] = values[n * size : (n + 1) * size]
        mix = jnp.concatenate(mixes, axis=0)
        rounded = mix.astype(BF16)
        mixtures[chunk, 0] = rounded
        mixtures[chunk, 1] = (mix - rounded.astype(F32)).astype(BF16)


def blocks_of(value):
    return [value[begin : begin + CAP] for begin in range(0, value.shape[0], CAP)]


def regroup_kernel(count, moves, *refs):
    values = [blocks_of(ref[...].astype(F32)) for ref in refs[:count]]
    for out, blocks in zip(refs[count:], moves):
        out[...] = jnp.concatenate([values[n][b] for n, b in blocks], axis=0).astype(out.dtype)


def sum_kernel(count, moves, *refs):
    values = [blocks_of(ref[...].astype(F32)) for ref in refs[:count]]
    for out, blocks in zip(refs[count:], moves):
        rows = [sum(values[n][b] for n, b in terms) for terms in blocks]
        out[...] = jnp.concatenate(rows, axis=0).astype(out.dtype)


def groups_of(owned):
    return [(0, 1)] + [(number + 1,) for number in range(1, owned)]


def order_of(info, owned):
    hot = jnp.max(info[...].astype(F32)).astype(jnp.int32)
    return [hot] + [n + (n >= hot).astype(jnp.int32) for n in range(owned - 1)]


def features_of(m, share):
    return pl.ds(pl.multiple_of((lax.axis_index("dp") ^ m) * share, share), share)


def projections(order, numbers, blocks, gate, up):
    owned = gate.shape[0]
    share = blocks[0].shape[1] // (owned + 1)
    for group, chunks in enumerate(groups_of(owned)):
        gate_value = up_value = None
        for m, block in zip(numbers, blocks):
            rows = jnp.concatenate([block[:, c * share : (c + 1) * share] for c in chunks], axis=0)
            gate_part = dot(rows, gate[order[group], features_of(m, share), :])
            up_part = dot(rows, up[order[group], features_of(m, share), :])
            gate_value = gate_part if gate_value is None else gate_value + gate_part
            up_value = up_part if up_value is None else up_value + up_part
        lines = block.shape[0]
        yield slice(chunks[0] * lines, (chunks[-1] + 1) * lines), gate_value, up_value


def first_kernel(numbers, info, gate, up, down, *refs):
    *blocks, gate_out, up_out = refs
    order = order_of(info, gate.shape[0])
    for place, gate_value, up_value in projections(order, numbers, blocks, gate, up):
        gate_out[place, :] = gate_value
        up_out[place, :] = up_value


def down_parts(order, numbers, hidden, down, outs):
    owned = down.shape[0]
    lines, wide = outs[0].shape
    share = wide // (owned + 1)
    for m, out in zip(numbers, outs):
        for group, chunks in enumerate(groups_of(owned)):
            rows = hidden[chunks[0] * lines : (chunks[-1] + 1) * lines, :]
            value = dot(rows, down[order[group], :, features_of(m, share)]).astype(out.dtype)
            for spot, chunk in enumerate(chunks):
                out[:, chunk * share : (chunk + 1) * share] = value[spot * lines : (spot + 1) * lines]


def second_kernel(numbers, out_number, info, gate, up, down, gate_in, up_in, *refs):
    *blocks, hidden, out = refs
    order = order_of(info, gate.shape[0])
    for place, gate_value, up_value in projections(order, numbers, blocks, gate, up):
        gate_value = gate_value + gate_in[place, :]
        up_value = up_value + up_in[place, :]
        hidden[place, :] = (jax.nn.silu(gate_value) * up_value).astype(BF16)
    down_parts(order, [out_number], hidden, down, [out])


def down_kernel(numbers, info, down, hidden, *outs):
    down_parts(order_of(info, down.shape[0]), numbers, hidden, down, outs)


def mixed_part(mixtures, pieces, columns):
    share = next(iter(pieces.values())).shape[1] // mixtures.shape[0]
    weights, rows = [], []
    for chunk in range(mixtures.shape[0]):
        for n, piece in pieces.items():
            size = piece.shape[0]
            values = piece[:, chunk * share + columns.start : chunk * share + columns.stop]
            for half in range(2):
                weights.append(mixtures[chunk, half, n * size : (n + 1) * size, :])
                rows.append(values)
    return dot_rows(jnp.concatenate(weights, axis=0), jnp.concatenate(rows, axis=0))


def mix_kernel(places, mixtures, *refs):
    *pieces, out, result, sems = refs
    share = out.shape[1]
    middle = share // 256 * 128
    copies = []
    for n, columns in enumerate((slice(0, middle), slice(middle, share))):
        value = mixed_part(mixtures, dict(zip(places, pieces)), columns)
        result[:, columns] = value.astype(result.dtype)
        copies.append(pltpu.make_async_copy(result.at[:, columns], out.at[:, columns], sems.at[n]))
        copies[-1].start()
    for copy in copies:
        copy.wait()


def call(kernel, outs, *args, specs=None, out_specs=None, scratch=(), flops=0):
    if specs:
        args = [
            pltpu.with_memory_space_constraint(a, s.memory_space) for a, s in zip(args, specs)
        ]
    return pl.pallas_call(
        kernel,
        out_shape=outs,
        in_specs=specs or [VMEM] * len(args),
        out_specs=out_specs or [VMEM] * len(outs),
        scratch_shapes=list(scratch),
        compiler_params=pltpu.CompilerParams(vmem_limit_bytes=LIMIT),
        cost_estimate=pl.CostEstimate(flops=flops + 1000, bytes_accessed=1000, transcendentals=0),
    )(*args)


def swapped(value, axis, mask):
    count = lax.axis_size(axis)
    return lax.ppermute(value, axis, [(source, source ^ mask) for source in range(count)])


def turned(value, low_step, across):
    parts = lax.axis_size("dp")
    if not across:
        return swapped(value, "expert", low_step)
    return swapped(value, ("expert", "dp"), low_step * parts + across)


def per_device(tokens, expert_ids, gate_weights, replica_plan, w_gate, w_up, w_down):
    owners = lax.axis_size("expert")
    parts = lax.axis_size("dp")
    owned, model_width, hidden_share = w_gate.shape
    tok_rows, share = tokens.shape
    choices = expert_ids.shape[1]
    chunks = owned + 1
    lines = owners * CAP
    wide = chunks * share
    low = 1 << ((owners.bit_length() - 1) // 2)
    high = owners // low
    high_steps = list(range(high - 1, -1, -1))
    ways_in = [high_steps[:1] + high_steps[-1:], high_steps[1:-1]]
    ways_in = [group for group in ways_in if group]
    ways_out = [high_steps[: high // 2], high_steps[high // 2 :]]
    shape = jax.ShapeDtypeStruct
    piece = shape((low * CAP, wide), BF16)
    whole = shape((lines, wide), BF16)

    def lot(group):
        return shape((len(group) * CAP, wide), BF16)

    *pieces, info, mixtures = call(
        functools.partial(route_kernel, owned, low, high_steps),
        [piece] * high
        + [shape((8, 128), jnp.int32), shape((chunks, 2, lines, tok_rows), BF16)],
        replica_plan, expert_ids.T, gate_weights.T, tokens,
        specs=[HBM] * 4,
        scratch=[
            pltpu.SMEM((owners,), jnp.int32),
            pltpu.VMEM((choices, tok_rows), jnp.int32),
            pltpu.VMEM((choices, tok_rows), F32),
            pltpu.VMEM((tok_rows, share), BF16),
            pltpu.VMEM((owners * owned, tok_rows), jnp.int32),
            pltpu.VMEM((owners * owned, tok_rows), F32),
            pltpu.SemaphoreType.DMA((4,)),
        ],
        flops=10**10,
    )
    arrived = {k: swapped(p, "expert", k * low) if k else p for k, p in zip(high_steps, pieces)}

    top = parts // 2
    rows, here, there = [], [], []
    for group in ways_in:
        lots = call(
            functools.partial(regroup_kernel, len(group), [
                [(n, m) for n in range(len(group))] for m in range(low)
            ]),
            [lot(group)] * low,
            *[arrived[k] for k in group],
        )
        there += [turned(value, m, top) for m, value in enumerate(lots)]
        here += [turned(value, m, 0) if m else value for m, value in enumerate(lots)]
        rows += [(k, m) for m in range(low) for k in group]
    moves = [(n, b) for n, value in enumerate(here) for b in range(value.shape[0] // CAP)]
    moves = [moves, [(n + len(here), b) for n, b in moves]]
    here, there = call(
        functools.partial(regroup_kernel, 2 * len(here), moves), [whole] * 2, *here, *there
    )
    blocks = {0: here, top: there}
    mask = top // 2
    while mask:
        for n in list(blocks):
            blocks[n ^ mask] = swapped(blocks[n], "dp", mask)
        mask //= 2
    first = [0, top]
    second = [n for n in range(parts) if n not in first]
    sums = [shape((chunks * lines, hidden_share), F32)] * 2
    gate_sum, up_sum = call(
        functools.partial(first_kernel, first),
        sums,
        info, w_gate, w_up, w_down, *[blocks[n] for n in first],
    )
    outs = {}
    hidden, outs[parts - 1] = call(
        functools.partial(second_kernel, second, parts - 1),
        [shape((chunks * lines, hidden_share), BF16), whole],
        info, w_gate, w_up, w_down, gate_sum, up_sum, *[blocks[n] for n in second],
    )
    far, near = list(range(top, parts - 1)), list(range(top))
    for numbers in (far, near):
        found = call(
            functools.partial(down_kernel, numbers), [whole] * len(numbers), info, w_down, hidden
        )
        outs |= dict(zip(numbers, found))

    def reduced(begin):
        found = {n: outs[n] for n in range(begin, begin + top)}
        mask = 1
        while 2 * mask < top:
            for n in [n for n in found if n & mask]:
                value = swapped(found.pop(n), "dp", mask)
                (found[n ^ mask],) = call(
                    functools.partial(sum_kernel, 2, [
                        [[(0, b), (1, b)] for b in range(len(rows))]
                    ]),
                    [whole], found[n ^ mask], value,
                )
            mask *= 2
        terms = [swapped(value, "dp", mask) if n & mask else value for n, value in found.items()]
        moves = [
            [[(t, rows.index((k, m))) for t in range(len(terms))] for k in group]
            for group in ways_out for m in range(low)
        ]
        sums = call(
            functools.partial(sum_kernel, len(terms), moves),
            [lot(group) for group in ways_out for m in range(low)],
            *terms,
        )
        return [sums[n : n + low] for n in range(0, len(sums), low)]

    back = {}
    for group, far_lots, near_lots in zip(ways_out, reduced(top), reduced(0)):
        terms = []
        for m in range(low):
            terms.append(turned(near_lots[m], m, 0) if m else near_lots[m])
            terms.append(turned(far_lots[m], m, top))
        moves = [[[(2 * m, n), (2 * m + 1, n)] for m in range(low)] for n in range(len(group))]
        totals = call(
            functools.partial(sum_kernel, 2 * low, moves), [piece] * len(group), *terms
        )
        for k, value in zip(group, totals):
            back[k] = swapped(value, "expert", k * low) if k else value
    (mixed_out,) = call(
        functools.partial(mix_kernel, range(high)),
        [shape((tok_rows, share), BF16)],
        mixtures, *[back[k] for k in high_steps],
        out_specs=[HBM],
        scratch=[pltpu.VMEM((tok_rows, share), BF16), pltpu.SemaphoreType.DMA((2,))],
    )
    return mixed_out


def solution(mesh):
    in_specs = (
        P("expert", "dp"),
        P("expert", None),
        P("expert", None),
        P(),
        P("expert", None, "dp"),
        P("expert", None, "dp"),
        P("expert", "dp", None),
    )
    out_specs = P("expert", "dp")
    return jax.shard_map(
        per_device, mesh=mesh, in_specs=in_specs, out_specs=out_specs, check_vma=False
    )
```

```python
import functools

import jax
import jax.numpy as jnp
from jax import lax
from jax.experimental import pallas as pl
from jax.experimental.pallas import tpu as pltpu
from jax.sharding import PartitionSpec as P

CAP = 8
F32 = jnp.float32
BF16 = jnp.bfloat16
HBM = pl.BlockSpec(memory_space=pltpu.HBM)
VMEM = pl.BlockSpec(memory_space=pltpu.VMEM)
LIMIT = 20 * 2**20


def dot(left, right):
    return jnp.dot(left, right, preferred_element_type=F32)


def dot_rows(left, right):
    return lax.dot_general(left, right, (((0,), (0,)), ((), ())), preferred_element_type=F32)


def route_kernel(owned, low, high_steps, plan_hbm, ids_hbm, gates_hbm, tokens_hbm, *refs):
    high = len(high_steps)
    pieces, (info, mixtures, plan, ids, gates, tokens, place, weight, sems) = refs[:high], refs[high:]
    sources = (plan_hbm, ids_hbm, gates_hbm, tokens_hbm)
    copies = [
        pltpu.make_async_copy(source, target, sems.at[n])
        for n, (source, target) in enumerate(zip(sources, (plan, ids, gates, tokens)))
    ]
    for copy in copies:
        copy.start()
    choices, tok_rows = ids.shape
    share = tokens.shape[1]
    owners = plan.shape[0]
    experts = owners * owned
    steps = [(k, m) for k in high_steps for m in range(low)]
    own_index = lax.axis_index("expert")
    row = lax.broadcasted_iota(jnp.int32, (tok_rows, tok_rows), 0)
    col = lax.broadcasted_iota(jnp.int32, (tok_rows, tok_rows), 1)
    earlier = (row < col).astype(F32).astype(BF16)
    expert = lax.broadcasted_iota(jnp.int32, (experts, tok_rows), 0)
    owner = expert // owned
    within = expert - owner * owned
    named = jnp.zeros((experts, tok_rows), F32)
    weights = jnp.zeros((experts, tok_rows), F32)
    hot = jnp.zeros((experts, tok_rows), jnp.int32)
    copies[0].wait()
    for host in range(owners):
        source = (host + owners // 2) % owners
        hot = jnp.where(owner == source, plan[host] - source * owned, hot)
    own_hot = plan[lax.rem(own_index + owners // 2, owners)] - own_index * owned
    info[...] = jnp.full(info.shape, own_hot, jnp.int32)
    copies[1].wait()
    copies[2].wait()
    for choice in range(choices):
        hit = expert == ids[choice : choice + 1, :]
        named = named + hit.astype(F32)
        weights = weights + jnp.where(hit, gates[choice : choice + 1, :], 0.0)
    weight[...] = weights
    rank = dot(named.astype(BF16), earlier).astype(jnp.int32)
    limit = jnp.where(within == hot, 2 * CAP, CAP)
    start = jnp.where(within == hot, 0, CAP * (1 + within + (within < hot).astype(jnp.int32)))
    place[...] = jnp.where((named > 0.0) & (rank < limit), start + rank, -1)
    slot = lax.broadcasted_iota(jnp.int32, (CAP, tok_rows), 0)
    zero = jnp.zeros((CAP, tok_rows), F32)
    copies[3].wait()
    for chunk in range(owned + 1):
        picks, mixes = [], []
        for k, m in steps:
            index = own_index ^ (k * low + m)
            pick, mix = zero, zero
            for number in range(owned):
                line = pl.ds(index * owned + number, 1)
                match = place[line, :] == slot + chunk * CAP
                pick = pick + match.astype(F32)
                mix = mix + jnp.where(match, weight[line, :], 0.0)
            picks.append(pick)
            mixes.append(mix)
        pick = jnp.concatenate(picks, axis=0).astype(BF16)
        values = dot(pick, tokens[...]).astype(BF16)
        size = low * CAP
        for n, piece in enumerate(pieces):
            piece[:, chunk * share : (chunk + 1) * share] = values[n * size : (n + 1) * size]
        mix = jnp.concatenate(mixes, axis=0)
        rounded = mix.astype(BF16)
        mixtures[chunk, 0] = rounded
        mixtures[chunk, 1] = (mix - rounded.astype(F32)).astype(BF16)


def blocks_of(value):
    return [value[begin : begin + CAP] for begin in range(0, value.shape[0], CAP)]


def regroup_kernel(count, moves, *refs):
    values = [blocks_of(ref[...].astype(F32)) for ref in refs[:count]]
    for out, blocks in zip(refs[count:], moves):
        out[...] = jnp.concatenate([values[n][b] for n, b in blocks], axis=0).astype(out.dtype)


def sum_kernel(count, moves, *refs):
    values = [blocks_of(ref[...].astype(F32)) for ref in refs[:count]]
    for out, blocks in zip(refs[count:], moves):
        rows = [sum(values[n][b] for n, b in terms) for terms in blocks]
        out[...] = jnp.concatenate(rows, axis=0).astype(out.dtype)


def groups_of(owned):
    return [(0, 1)] + [(number + 1,) for number in range(1, owned)]


def order_of(info, owned):
    hot = jnp.max(info[...].astype(F32)).astype(jnp.int32)
    return [hot] + [n + (n >= hot).astype(jnp.int32) for n in range(owned - 1)]


def features_of(m, share):
    return pl.ds(pl.multiple_of((lax.axis_index("dp") ^ m) * share, share), share)


def projections(order, numbers, blocks, gate, up):
    owned = gate.shape[0]
    share = blocks[0].shape[1] // (owned + 1)
    for group, chunks in enumerate(groups_of(owned)):
        gate_value = up_value = None
        for m, block in zip(numbers, blocks):
            rows = jnp.concatenate([block[:, c * share : (c + 1) * share] for c in chunks], axis=0)
            gate_part = dot(rows, gate[order[group], features_of(m, share), :])
            up_part = dot(rows, up[order[group], features_of(m, share), :])
            gate_value = gate_part if gate_value is None else gate_value + gate_part
            up_value = up_part if up_value is None else up_value + up_part
        lines = block.shape[0]
        yield slice(chunks[0] * lines, (chunks[-1] + 1) * lines), gate_value, up_value


def first_kernel(numbers, info, gate, up, down, *refs):
    *blocks, gate_out, up_out = refs
    order = order_of(info, gate.shape[0])
    for place, gate_value, up_value in projections(order, numbers, blocks, gate, up):
        gate_out[place, :] = gate_value
        up_out[place, :] = up_value


def down_parts(order, numbers, hidden, down, outs):
    owned = down.shape[0]
    lines, wide = outs[0].shape
    share = wide // (owned + 1)
    for m, out in zip(numbers, outs):
        for group, chunks in enumerate(groups_of(owned)):
            rows = hidden[chunks[0] * lines : (chunks[-1] + 1) * lines, :]
            value = dot(rows, down[order[group], :, features_of(m, share)]).astype(out.dtype)
            for spot, chunk in enumerate(chunks):
                out[:, chunk * share : (chunk + 1) * share] = value[spot * lines : (spot + 1) * lines]


def second_kernel(numbers, out_number, info, gate, up, down, gate_in, up_in, *refs):
    *blocks, hidden, out = refs
    order = order_of(info, gate.shape[0])
    for place, gate_value, up_value in projections(order, numbers, blocks, gate, up):
        gate_value = gate_value + gate_in[place, :]
        up_value = up_value + up_in[place, :]
        hidden[place, :] = (jax.nn.silu(gate_value) * up_value).astype(BF16)
    down_parts(order, [out_number], hidden, down, [out])


def down_kernel(numbers, info, down, hidden, *outs):
    down_parts(order_of(info, down.shape[0]), numbers, hidden, down, outs)


def mixed_part(mixtures, pieces, columns):
    share = next(iter(pieces.values())).shape[1] // mixtures.shape[0]
    weights, rows = [], []
    for chunk in range(mixtures.shape[0]):
        for n, piece in pieces.items():
            size = piece.shape[0]
            values = piece[:, chunk * share + columns.start : chunk * share + columns.stop]
            for half in range(2):
                weights.append(mixtures[chunk, half, n * size : (n + 1) * size, :])
                rows.append(values)
    return dot_rows(jnp.concatenate(weights, axis=0), jnp.concatenate(rows, axis=0))


def mix_kernel(places, mixtures, *refs):
    *pieces, out, result, sems = refs
    share = out.shape[1]
    middle = share // 256 * 128
    copies = []
    for n, columns in enumerate((slice(0, middle), slice(middle, share))):
        value = mixed_part(mixtures, dict(zip(places, pieces)), columns)
        result[:, columns] = value.astype(result.dtype)
        copies.append(pltpu.make_async_copy(result.at[:, columns], out.at[:, columns], sems.at[n]))
        copies[-1].start()
    for copy in copies:
        copy.wait()


def call(kernel, outs, *args, specs=None, out_specs=None, scratch=(), flops=0):
    if specs:
        args = [
            pltpu.with_memory_space_constraint(a, s.memory_space) for a, s in zip(args, specs)
        ]
    return pl.pallas_call(
        kernel,
        out_shape=outs,
        in_specs=specs or [VMEM] * len(args),
        out_specs=out_specs or [VMEM] * len(outs),
        scratch_shapes=list(scratch),
        compiler_params=pltpu.CompilerParams(vmem_limit_bytes=LIMIT),
        cost_estimate=pl.CostEstimate(flops=flops + 1000, bytes_accessed=1000, transcendentals=0),
    )(*args)


def swapped(value, axis, mask):
    count = lax.axis_size(axis)
    return lax.ppermute(value, axis, [(source, source ^ mask) for source in range(count)])


def turned(value, low_step, across):
    parts = lax.axis_size("dp")
    if not across:
        return swapped(value, "expert", low_step)
    return swapped(value, ("expert", "dp"), low_step * parts + across)


def per_device(tokens, expert_ids, gate_weights, replica_plan, w_gate, w_up, w_down):
    owners = lax.axis_size("expert")
    parts = lax.axis_size("dp")
    owned, model_width, hidden_share = w_gate.shape
    tok_rows, share = tokens.shape
    choices = expert_ids.shape[1]
    chunks = owned + 1
    lines = owners * CAP
    wide = chunks * share
    low = 1 << ((owners.bit_length() - 1) // 2)
    high = owners // low
    high_steps = list(range(high - 1, -1, -1))
    ways_in = [high_steps[:1] + high_steps[-1:], high_steps[1:-1]]
    ways_in = [group for group in ways_in if group]
    ways_out = [high_steps[: high // 2], high_steps[high // 2 :]]
    shape = jax.ShapeDtypeStruct
    piece = shape((low * CAP, wide), BF16)
    whole = shape((lines, wide), BF16)

    def lot(group):
        return shape((len(group) * CAP, wide), BF16)

    *pieces, info, mixtures = call(
        functools.partial(route_kernel, owned, low, high_steps),
        [piece] * high
        + [shape((8, 128), jnp.int32), shape((chunks, 2, lines, tok_rows), BF16)],
        replica_plan, expert_ids.T, gate_weights.T, tokens,
        specs=[HBM] * 4,
        scratch=[
            pltpu.SMEM((owners,), jnp.int32),
            pltpu.VMEM((choices, tok_rows), jnp.int32),
            pltpu.VMEM((choices, tok_rows), F32),
            pltpu.VMEM((tok_rows, share), BF16),
            pltpu.VMEM((owners * owned, tok_rows), jnp.int32),
            pltpu.VMEM((owners * owned, tok_rows), F32),
            pltpu.SemaphoreType.DMA((4,)),
        ],
        flops=10**10,
    )
    arrived = {k: swapped(p, "expert", k * low) if k else p for k, p in zip(high_steps, pieces)}

    top = parts // 2
    rows, here, there = [], [], []
    for group in ways_in:
        lots = call(
            functools.partial(regroup_kernel, len(group), [
                [(n, m) for n in range(len(group))] for m in range(low)
            ]),
            [lot(group)] * low,
            *[arrived[k] for k in group],
        )
        there += [turned(value, m, top) for m, value in enumerate(lots)]
        here += [turned(value, m, 0) if m else value for m, value in enumerate(lots)]
        rows += [(k, m) for m in range(low) for k in group]
    moves = [(n, b) for n, value in enumerate(here) for b in range(value.shape[0] // CAP)]
    here, there = (
        call(functools.partial(regroup_kernel, len(lots), [moves]), [whole], *lots)[0]
        for lots in (here, there)
    )
    blocks = {0: here, top: there}
    mask = top // 2
    while mask:
        for n in list(blocks):
            blocks[n ^ mask] = swapped(blocks[n], "dp", mask)
        mask //= 2
    first = list(range(top + 1))
    second = [n for n in range(parts) if n not in first]
    sums = [shape((chunks * lines, hidden_share), F32)] * 2
    gate_sum, up_sum = call(
        functools.partial(first_kernel, first),
        sums,
        info, w_gate, w_up, w_down, *[blocks[n] for n in first],
    )
    outs = {}
    hidden, outs[parts - 1] = call(
        functools.partial(second_kernel, second, parts - 1),
        [shape((chunks * lines, hidden_share), BF16), whole],
        info, w_gate, w_up, w_down, gate_sum, up_sum, *[blocks[n] for n in second],
    )
    far, near = list(range(top, parts - 1)), list(range(top))
    for numbers in (far, near):
        found = call(
            functools.partial(down_kernel, numbers), [whole] * len(numbers), info, w_down, hidden
        )
        outs |= dict(zip(numbers, found))

    def reduced(begin):
        found = {n: outs[n] for n in range(begin, begin + top)}
        mask = 1
        while 2 * mask < top:
            for n in [n for n in found if n & mask]:
                value = swapped(found.pop(n), "dp", mask)
                (found[n ^ mask],) = call(
                    functools.partial(sum_kernel, 2, [
                        [[(0, b), (1, b)] for b in range(len(rows))]
                    ]),
                    [whole], found[n ^ mask], value,
                )
            mask *= 2
        return [swapped(value, "dp", mask) if n & mask else value for n, value in found.items()]

    def summed(wanted, *terms):
        values, moves, kinds = [value for both in terms for value in both], [], []
        for group in ways_out:
            for t, steps in wanted:
                places = [t * len(terms[t]) + n for n in range(len(terms[t]))]
                for m in steps:
                    moves.append([[(n, rows.index((k, m))) for n in places] for k in group])
                    kinds.append(lot(group))
        return call(functools.partial(sum_kernel, len(values), moves), kinds, *values)

    far_terms, near_terms = reduced(top), reduced(0)
    across = summed([(0, [0])], far_terms)
    others = summed([(0, range(low)), (1, range(1, low))], near_terms, far_terms)
    lots_out = [
        [across[g], *others[g * (2 * low - 1) : (g + 1) * (2 * low - 1)]]
        for g in range(len(ways_out))
    ]
    back = {}
    for group, lots in zip(ways_out, lots_out):
        terms, near_lots, far_lots = [], lots[1 : 1 + low], [lots[0], *lots[1 + low :]]
        for m in range(low):
            terms.append(turned(near_lots[m], m, 0) if m else near_lots[m])
            terms.append(turned(far_lots[m], m, top))
        moves = [[[(2 * m, n), (2 * m + 1, n)] for m in range(low)] for n in range(len(group))]
        totals = call(
            functools.partial(sum_kernel, 2 * low, moves), [piece] * len(group), *terms
        )
        for k, value in zip(group, totals):
            back[k] = swapped(value, "expert", k * low) if k else value
    (mixed_out,) = call(
        functools.partial(mix_kernel, range(high)),
        [shape((tok_rows, share), BF16)],
        mixtures, *[back[k] for k in high_steps],
        out_specs=[HBM],
        scratch=[pltpu.VMEM((tok_rows, share), BF16), pltpu.SemaphoreType.DMA((2,))],
    )
    return mixed_out


def solution(mesh):
    in_specs = (
        P("expert", "dp"),
        P("expert", None),
        P("expert", None),
        P(),
        P("expert", None, "dp"),
        P("expert", None, "dp"),
        P("expert", "dp", None),
    )
    out_specs = P("expert", "dp")
    return jax.shard_map(
        per_device, mesh=mesh, in_specs=in_specs, out_specs=out_specs, check_vma=False
    )
```

```python
import functools

import jax
import jax.numpy as jnp
from jax import lax
from jax.experimental import pallas as pl
from jax.experimental.pallas import tpu as pltpu
from jax.sharding import PartitionSpec as P

CAP = 8
F32 = jnp.float32
BF16 = jnp.bfloat16
HBM = pl.BlockSpec(memory_space=pltpu.HBM)
VMEM = pl.BlockSpec(memory_space=pltpu.VMEM)
LIMIT = 20 * 2**20


def dot(left, right):
    return jnp.dot(left, right, preferred_element_type=F32)


def dot_rows(left, right):
    return lax.dot_general(left, right, (((0,), (0,)), ((), ())), preferred_element_type=F32)


def dispatch(owned, low, high_steps, place, tokens, pieces):
    tok_rows, share = tokens.shape
    own_index = lax.axis_index("expert")
    slot = lax.broadcasted_iota(jnp.int32, (CAP, tok_rows), 0)
    size = low * CAP
    for chunk in range(owned + 1):
        picks = []
        for k, m in [(k, m) for k in high_steps for m in range(low)]:
            pick = jnp.zeros((CAP, tok_rows), F32)
            for number in range(owned):
                line = pl.ds((own_index ^ (k * low + m)) * owned + number, 1)
                pick = pick + (place[line, :] == slot + chunk * CAP).astype(F32)
            picks.append(pick)
        values = dot(jnp.concatenate(picks, axis=0).astype(BF16), tokens[...]).astype(BF16)
        for n, piece in enumerate(pieces):
            piece[:, chunk * share : (chunk + 1) * share] = values[n * size : (n + 1) * size]


def route_kernel(owned, low, high_steps, plan_hbm, ids_hbm, gates_hbm, tokens_hbm, *refs):
    pieces = refs[: len(high_steps)]
    info, place, weight, tokens, plan, ids, gates, sems = refs[len(high_steps) :]
    sources = (plan_hbm, ids_hbm, gates_hbm, tokens_hbm)
    copies = [
        pltpu.make_async_copy(source, target, sems.at[n])
        for n, (source, target) in enumerate(zip(sources, (plan, ids, gates, tokens)))
    ]
    for copy in copies:
        copy.start()
    choices, tok_rows = ids.shape
    owners = plan.shape[0]
    experts = owners * owned
    own_index = lax.axis_index("expert")
    row = lax.broadcasted_iota(jnp.int32, (tok_rows, tok_rows), 0)
    col = lax.broadcasted_iota(jnp.int32, (tok_rows, tok_rows), 1)
    earlier = (row < col).astype(F32).astype(BF16)
    expert = lax.broadcasted_iota(jnp.int32, (experts, tok_rows), 0)
    owner = expert // owned
    within = expert - owner * owned
    named = jnp.zeros((experts, tok_rows), F32)
    weights = jnp.zeros((experts, tok_rows), F32)
    hot = jnp.zeros((experts, tok_rows), jnp.int32)
    copies[0].wait()
    for host in range(owners):
        source = (host + owners // 2) % owners
        hot = jnp.where(owner == source, plan[host] - source * owned, hot)
    own_hot = plan[lax.rem(own_index + owners // 2, owners)] - own_index * owned
    info[...] = jnp.full(info.shape, own_hot, jnp.int32)
    copies[1].wait()
    copies[2].wait()
    for choice in range(choices):
        hit = expert == ids[choice : choice + 1, :]
        named = named + hit.astype(F32)
        weights = weights + jnp.where(hit, gates[choice : choice + 1, :], 0.0)
    weight[...] = weights
    rank = dot(named.astype(BF16), earlier).astype(jnp.int32)
    limit = jnp.where(within == hot, 2 * CAP, CAP)
    start = jnp.where(within == hot, 0, CAP * (1 + within + (within < hot).astype(jnp.int32)))
    place[...] = jnp.where((named > 0.0) & (rank < limit), start + rank, -1)
    copies[3].wait()
    dispatch(owned, low, high_steps, place, tokens, pieces)


def rest_kernel(owned, low, rest_steps, high_steps, place, weight, tokens, *refs):
    *pieces, mixtures = refs
    dispatch(owned, low, rest_steps, place, tokens, pieces)
    own_index = lax.axis_index("expert")
    slot = lax.broadcasted_iota(jnp.int32, (CAP, place.shape[1]), 0)
    for chunk in range(owned + 1):
        mixes = []
        for k, m in [(k, m) for k in high_steps for m in range(low)]:
            mix = jnp.zeros(slot.shape, F32)
            for number in range(owned):
                line = pl.ds((own_index ^ (k * low + m)) * owned + number, 1)
                mix = mix + jnp.where(place[line, :] == slot + chunk * CAP, weight[line, :], 0.0)
            mixes.append(mix)
        mix = jnp.concatenate(mixes, axis=0)
        rounded = mix.astype(BF16)
        mixtures[chunk, 0] = rounded
        mixtures[chunk, 1] = (mix - rounded.astype(F32)).astype(BF16)


def blocks_of(value):
    return [value[begin : begin + CAP] for begin in range(0, value.shape[0], CAP)]


def regroup_kernel(count, moves, *refs):
    values = [blocks_of(ref[...].astype(F32)) for ref in refs[:count]]
    for out, blocks in zip(refs[count:], moves):
        out[...] = jnp.concatenate([values[n][b] for n, b in blocks], axis=0).astype(out.dtype)


def sum_kernel(count, moves, *refs):
    values = [blocks_of(ref[...].astype(F32)) for ref in refs[:count]]
    for out, blocks in zip(refs[count:], moves):
        rows = [sum(values[n][b] for n, b in terms) for terms in blocks]
        out[...] = jnp.concatenate(rows, axis=0).astype(out.dtype)


def groups_of(owned):
    return [(0, 1)] + [(number + 1,) for number in range(1, owned)]


def order_of(info, owned):
    hot = jnp.max(info[...].astype(F32)).astype(jnp.int32)
    return [hot] + [n + (n >= hot).astype(jnp.int32) for n in range(owned - 1)]


def features_of(m, share):
    return pl.ds(pl.multiple_of((lax.axis_index("dp") ^ m) * share, share), share)


def projections(order, numbers, blocks, gate, up):
    owned = gate.shape[0]
    share = blocks[0].shape[1] // (owned + 1)
    for group, chunks in enumerate(groups_of(owned)):
        gate_value = up_value = None
        for m, block in zip(numbers, blocks):
            rows = jnp.concatenate([block[:, c * share : (c + 1) * share] for c in chunks], axis=0)
            gate_part = dot(rows, gate[order[group], features_of(m, share), :])
            up_part = dot(rows, up[order[group], features_of(m, share), :])
            gate_value = gate_part if gate_value is None else gate_value + gate_part
            up_value = up_part if up_value is None else up_value + up_part
        lines = block.shape[0]
        yield slice(chunks[0] * lines, (chunks[-1] + 1) * lines), gate_value, up_value


def first_kernel(numbers, info, gate, up, down, *refs):
    *blocks, gate_out, up_out = refs
    order = order_of(info, gate.shape[0])
    for place, gate_value, up_value in projections(order, numbers, blocks, gate, up):
        gate_out[place, :] = gate_value
        up_out[place, :] = up_value


def down_parts(order, numbers, hidden, down, outs):
    owned = down.shape[0]
    lines, wide = outs[0].shape
    share = wide // (owned + 1)
    for m, out in zip(numbers, outs):
        for group, chunks in enumerate(groups_of(owned)):
            rows = hidden[chunks[0] * lines : (chunks[-1] + 1) * lines, :]
            value = dot(rows, down[order[group], :, features_of(m, share)]).astype(out.dtype)
            for spot, chunk in enumerate(chunks):
                out[:, chunk * share : (chunk + 1) * share] = value[spot * lines : (spot + 1) * lines]


def second_kernel(numbers, out_number, info, gate, up, down, gate_in, up_in, *refs):
    *blocks, hidden, out = refs
    order = order_of(info, gate.shape[0])
    for place, gate_value, up_value in projections(order, numbers, blocks, gate, up):
        gate_value = gate_value + gate_in[place, :]
        up_value = up_value + up_in[place, :]
        hidden[place, :] = (jax.nn.silu(gate_value) * up_value).astype(BF16)
    down_parts(order, [out_number], hidden, down, [out])


def down_kernel(numbers, info, down, hidden, *outs):
    down_parts(order_of(info, down.shape[0]), numbers, hidden, down, outs)


def mixed_part(mixtures, pieces, columns):
    share = next(iter(pieces.values())).shape[1] // mixtures.shape[0]
    weights, rows = [], []
    for chunk in range(mixtures.shape[0]):
        for n, piece in pieces.items():
            size = piece.shape[0]
            values = piece[:, chunk * share + columns.start : chunk * share + columns.stop]
            for half in range(2):
                weights.append(mixtures[chunk, half, n * size : (n + 1) * size, :])
                rows.append(values)
    return dot_rows(jnp.concatenate(weights, axis=0), jnp.concatenate(rows, axis=0))


def mix_kernel(places, mixtures, *refs):
    *pieces, out, result, sems = refs
    share = out.shape[1]
    middle = share // 256 * 128
    copies = []
    for n, columns in enumerate((slice(0, middle), slice(middle, share))):
        value = mixed_part(mixtures, dict(zip(places, pieces)), columns)
        result[:, columns] = value.astype(result.dtype)
        copies.append(pltpu.make_async_copy(result.at[:, columns], out.at[:, columns], sems.at[n]))
        copies[-1].start()
    for copy in copies:
        copy.wait()


def call(kernel, outs, *args, specs=None, out_specs=None, scratch=(), flops=0):
    if specs:
        args = [
            pltpu.with_memory_space_constraint(a, s.memory_space) for a, s in zip(args, specs)
        ]
    return pl.pallas_call(
        kernel,
        out_shape=outs,
        in_specs=specs or [VMEM] * len(args),
        out_specs=out_specs or [VMEM] * len(outs),
        scratch_shapes=list(scratch),
        compiler_params=pltpu.CompilerParams(vmem_limit_bytes=LIMIT),
        cost_estimate=pl.CostEstimate(flops=flops + 1000, bytes_accessed=1000, transcendentals=0),
    )(*args)


def swapped(value, axis, mask):
    count = lax.axis_size(axis)
    return lax.ppermute(value, axis, [(source, source ^ mask) for source in range(count)])


def turned(value, low_step, across):
    parts = lax.axis_size("dp")
    if not across:
        return swapped(value, "expert", low_step)
    return swapped(value, ("expert", "dp"), low_step * parts + across)


def per_device(tokens, expert_ids, gate_weights, replica_plan, w_gate, w_up, w_down):
    owners = lax.axis_size("expert")
    parts = lax.axis_size("dp")
    owned, model_width, hidden_share = w_gate.shape
    tok_rows, share = tokens.shape
    choices = expert_ids.shape[1]
    chunks = owned + 1
    lines = owners * CAP
    wide = chunks * share
    low = 1 << ((owners.bit_length() - 1) // 2)
    high = owners // low
    high_steps = list(range(high - 1, -1, -1))
    ways_in = [high_steps[:1] + high_steps[-1:], high_steps[1:-1]]
    ways_in = [group for group in ways_in if group]
    ways_out = [high_steps[: high // 2], high_steps[high // 2 :]]
    shape = jax.ShapeDtypeStruct
    piece = shape((low * CAP, wide), BF16)
    whole = shape((lines, wide), BF16)

    def lot(group):
        return shape((len(group) * CAP, wide), BF16)

    first_steps, rest_steps = high_steps[: high // 2], high_steps[high // 2 :]
    experts = owners * owned
    *pieces, info, place, weight, tokens_here = call(
        functools.partial(route_kernel, owned, low, first_steps),
        [piece] * len(first_steps)
        + [shape((8, 128), jnp.int32)]
        + [shape((experts, tok_rows), kind) for kind in (jnp.int32, F32)]
        + [shape(tokens.shape, BF16)],
        replica_plan, expert_ids.T, gate_weights.T, tokens,
        specs=[HBM] * 4,
        scratch=[
            pltpu.SMEM((owners,), jnp.int32),
            pltpu.VMEM((choices, tok_rows), jnp.int32),
            pltpu.VMEM((choices, tok_rows), F32),
            pltpu.SemaphoreType.DMA((4,)),
        ],
        flops=10**10,
    )
    *others, mixtures = call(
        functools.partial(rest_kernel, owned, low, rest_steps, high_steps),
        [piece] * len(rest_steps) + [shape((chunks, 2, lines, tok_rows), BF16)],
        place, weight, tokens_here,
    )
    pieces += others
    arrived = {k: swapped(p, "expert", k * low) if k else p for k, p in zip(high_steps, pieces)}

    top = parts // 2
    rows, here, there = [], [], []
    for group in ways_in:
        lots = call(
            functools.partial(regroup_kernel, len(group), [
                [(n, m) for n in range(len(group))] for m in range(low)
            ]),
            [lot(group)] * low,
            *[arrived[k] for k in group],
        )
        there += [turned(value, m, top) for m, value in enumerate(lots)]
        here += [turned(value, m, 0) if m else value for m, value in enumerate(lots)]
        rows += [(k, m) for m in range(low) for k in group]
    moves = [(n, b) for n, value in enumerate(here) for b in range(value.shape[0] // CAP)]
    there, here = (
        call(functools.partial(regroup_kernel, len(lots), [moves]), [whole], *lots)[0]
        for lots in (there, here)
    )
    blocks = {top: there, 0: here}
    mask = top // 2
    while mask:
        for n in list(blocks):
            blocks[n ^ mask] = swapped(blocks[n], "dp", mask)
        mask //= 2
    first = [0, *range(top, parts)]
    second = [n for n in range(parts) if n not in first]
    sums = [shape((chunks * lines, hidden_share), F32)] * 2
    gate_sum, up_sum = call(
        functools.partial(first_kernel, first),
        sums,
        info, w_gate, w_up, w_down, *[blocks[n] for n in first],
    )
    outs = {}
    hidden, outs[parts - 1] = call(
        functools.partial(second_kernel, second, parts - 1),
        [shape((chunks * lines, hidden_share), BF16), whole],
        info, w_gate, w_up, w_down, gate_sum, up_sum, *[blocks[n] for n in second],
    )
    far, near = list(range(top, parts - 1)), list(range(top))
    for numbers in (far, near):
        found = call(
            functools.partial(down_kernel, numbers), [whole] * len(numbers), info, w_down, hidden
        )
        outs |= dict(zip(numbers, found))

    def reduced(begin):
        found = {n: outs[n] for n in range(begin, begin + top)}
        mask = 1
        while 2 * mask < top:
            for n in [n for n in found if n & mask]:
                value = swapped(found.pop(n), "dp", mask)
                (found[n ^ mask],) = call(
                    functools.partial(sum_kernel, 2, [
                        [[(0, b), (1, b)] for b in range(len(rows))]
                    ]),
                    [whole], found[n ^ mask], value,
                )
            mask *= 2
        return [swapped(value, "dp", mask) if n & mask else value for n, value in found.items()]

    def summed(wanted, *terms):
        values, moves, kinds = [value for both in terms for value in both], [], []
        for group in ways_out:
            for t, steps in wanted:
                places = [t * len(terms[t]) + n for n in range(len(terms[t]))]
                for m in steps:
                    moves.append([[(n, rows.index((k, m))) for n in places] for k in group])
                    kinds.append(lot(group))
        return call(functools.partial(sum_kernel, len(values), moves), kinds, *values)

    far_terms, near_terms = reduced(top), reduced(0)
    across = summed([(0, [0])], far_terms)
    others = summed([(0, range(low)), (1, range(1, low))], near_terms, far_terms)
    lots_out = [
        [across[g], *others[g * (2 * low - 1) : (g + 1) * (2 * low - 1)]]
        for g in range(len(ways_out))
    ]
    back = {}
    for group, lots in zip(ways_out, lots_out):
        terms, near_lots, far_lots = [], lots[1 : 1 + low], [lots[0], *lots[1 + low :]]
        for m in range(low):
            terms.append(turned(near_lots[m], m, 0) if m else near_lots[m])
            terms.append(turned(far_lots[m], m, top))
        moves = [[[(2 * m, n), (2 * m + 1, n)] for m in range(low)] for n in range(len(group))]
        totals = call(
            functools.partial(sum_kernel, 2 * low, moves), [piece] * len(group), *terms
        )
        for k, value in zip(group, totals):
            back[k] = swapped(value, "expert", k * low) if k else value
    (mixed_out,) = call(
        functools.partial(mix_kernel, range(high)),
        [shape((tok_rows, share), BF16)],
        mixtures, *[back[k] for k in high_steps],
        out_specs=[HBM],
        scratch=[pltpu.VMEM((tok_rows, share), BF16), pltpu.SemaphoreType.DMA((2,))],
    )
    return mixed_out


def solution(mesh):
    in_specs = (
        P("expert", "dp"),
        P("expert", None),
        P("expert", None),
        P(),
        P("expert", None, "dp"),
        P("expert", None, "dp"),
        P("expert", "dp", None),
    )
    out_specs = P("expert", "dp")
    return jax.shard_map(
        per_device, mesh=mesh, in_specs=in_specs, out_specs=out_specs, check_vma=False
    )
```

```python
import functools

import jax
import jax.numpy as jnp
from jax import lax
from jax.experimental import pallas as pl
from jax.experimental.pallas import tpu as pltpu
from jax.sharding import PartitionSpec as P

CAP = 8
F32 = jnp.float32
BF16 = jnp.bfloat16
HBM = pl.BlockSpec(memory_space=pltpu.HBM)
VMEM = pl.BlockSpec(memory_space=pltpu.VMEM)
LIMIT = 20 * 2**20


def dot(left, right):
    return jnp.dot(left, right, preferred_element_type=F32)


def dot_rows(left, right):
    return lax.dot_general(left, right, (((0,), (0,)), ((), ())), preferred_element_type=F32)


def dispatch(owned, low, high_steps, place, tokens, pieces):
    tok_rows, share = tokens.shape
    own_index = lax.axis_index("expert")
    slot = lax.broadcasted_iota(jnp.int32, (CAP, tok_rows), 0)
    size = low * CAP
    picks = []
    for chunk in range(owned + 1):
        for k, m in [(k, m) for k in high_steps for m in range(low)]:
            pick = jnp.zeros((CAP, tok_rows), F32)
            for number in range(owned):
                line = pl.ds((own_index ^ (k * low + m)) * owned + number, 1)
                pick = pick + (place[line, :] == slot + chunk * CAP).astype(F32)
            picks.append(pick)
    values = dot(jnp.concatenate(picks, axis=0).astype(BF16), tokens[...]).astype(BF16)
    for chunk in range(owned + 1):
        for n, piece in enumerate(pieces):
            begin = (chunk * len(pieces) + n) * size
            piece[:, chunk * share : (chunk + 1) * share] = values[begin : begin + size]


def route_kernel(owned, low, high_steps, plan_hbm, ids_hbm, gates_hbm, tokens_hbm, *refs):
    pieces = refs[: len(high_steps)]
    info, place, weight, tokens, plan, ids, gates, sems = refs[len(high_steps) :]
    sources = (plan_hbm, ids_hbm, gates_hbm, tokens_hbm)
    copies = [
        pltpu.make_async_copy(source, target, sems.at[n])
        for n, (source, target) in enumerate(zip(sources, (plan, ids, gates, tokens)))
    ]
    for copy in copies:
        copy.start()
    choices, tok_rows = ids.shape
    owners = plan.shape[0]
    experts = owners * owned
    own_index = lax.axis_index("expert")
    row = lax.broadcasted_iota(jnp.int32, (tok_rows, tok_rows), 0)
    col = lax.broadcasted_iota(jnp.int32, (tok_rows, tok_rows), 1)
    earlier = (row < col).astype(F32).astype(BF16)
    expert = lax.broadcasted_iota(jnp.int32, (experts, tok_rows), 0)
    owner = expert // owned
    within = expert - owner * owned
    named = jnp.zeros((experts, tok_rows), F32)
    weights = jnp.zeros((experts, tok_rows), F32)
    hot = jnp.zeros((experts, tok_rows), jnp.int32)
    copies[0].wait()
    for host in range(owners):
        source = (host + owners // 2) % owners
        hot = jnp.where(owner == source, plan[host] - source * owned, hot)
    own_hot = plan[lax.rem(own_index + owners // 2, owners)] - own_index * owned
    info[...] = jnp.full(info.shape, own_hot, jnp.int32)
    copies[1].wait()
    copies[2].wait()
    for choice in range(choices):
        hit = expert == ids[choice : choice + 1, :]
        named = named + hit.astype(F32)
        weights = weights + jnp.where(hit, gates[choice : choice + 1, :], 0.0)
    weight[...] = weights
    rank = dot(named.astype(BF16), earlier).astype(jnp.int32)
    limit = jnp.where(within == hot, 2 * CAP, CAP)
    start = jnp.where(within == hot, 0, CAP * (1 + within + (within < hot).astype(jnp.int32)))
    place[...] = jnp.where((named > 0.0) & (rank < limit), start + rank, -1)
    copies[3].wait()
    dispatch(owned, low, high_steps, place, tokens, pieces)


def rest_kernel(owned, low, rest_steps, high_steps, place, weight, tokens, *refs):
    *pieces, mixtures = refs
    dispatch(owned, low, rest_steps, place, tokens, pieces)
    own_index = lax.axis_index("expert")
    slot = lax.broadcasted_iota(jnp.int32, (CAP, place.shape[1]), 0)
    for chunk in range(owned + 1):
        mixes = []
        for k, m in [(k, m) for k in high_steps for m in range(low)]:
            mix = jnp.zeros(slot.shape, F32)
            for number in range(owned):
                line = pl.ds((own_index ^ (k * low + m)) * owned + number, 1)
                mix = mix + jnp.where(place[line, :] == slot + chunk * CAP, weight[line, :], 0.0)
            mixes.append(mix)
        mix = jnp.concatenate(mixes, axis=0)
        rounded = mix.astype(BF16)
        mixtures[chunk, 0] = rounded
        mixtures[chunk, 1] = (mix - rounded.astype(F32)).astype(BF16)


def blocks_of(value):
    return [value[begin : begin + CAP] for begin in range(0, value.shape[0], CAP)]


def regroup_kernel(count, moves, *refs):
    values = [blocks_of(ref[...].astype(F32)) for ref in refs[:count]]
    for out, blocks in zip(refs[count:], moves):
        out[...] = jnp.concatenate([values[n][b] for n, b in blocks], axis=0).astype(out.dtype)


def sum_kernel(count, moves, *refs):
    values = [blocks_of(ref[...].astype(F32)) for ref in refs[:count]]
    for out, blocks in zip(refs[count:], moves):
        rows = [sum(values[n][b] for n, b in terms) for terms in blocks]
        out[...] = jnp.concatenate(rows, axis=0).astype(out.dtype)


def groups_of(owned):
    return [(0, 1)] + [(number + 1,) for number in range(1, owned)]


def order_of(info, owned):
    hot = jnp.max(info[...].astype(F32)).astype(jnp.int32)
    return [hot] + [n + (n >= hot).astype(jnp.int32) for n in range(owned - 1)]


def features_of(m, share):
    return pl.ds(pl.multiple_of((lax.axis_index("dp") ^ m) * share, share), share)


def projections(order, numbers, blocks, gate, up):
    owned = gate.shape[0]
    share = blocks[0].shape[1] // (owned + 1)
    for group, chunks in enumerate(groups_of(owned)):
        gate_value = up_value = None
        for m, block in zip(numbers, blocks):
            rows = jnp.concatenate([block[:, c * share : (c + 1) * share] for c in chunks], axis=0)
            gate_part = dot(rows, gate[order[group], features_of(m, share), :])
            up_part = dot(rows, up[order[group], features_of(m, share), :])
            gate_value = gate_part if gate_value is None else gate_value + gate_part
            up_value = up_part if up_value is None else up_value + up_part
        lines = block.shape[0]
        yield slice(chunks[0] * lines, (chunks[-1] + 1) * lines), gate_value, up_value


def first_kernel(numbers, info, gate, up, down, *refs):
    *blocks, gate_out, up_out = refs
    order = order_of(info, gate.shape[0])
    for place, gate_value, up_value in projections(order, numbers, blocks, gate, up):
        gate_out[place, :] = gate_value
        up_out[place, :] = up_value


def down_parts(order, numbers, hidden, down, outs):
    owned = down.shape[0]
    lines, wide = outs[0].shape
    share = wide // (owned + 1)
    for m, out in zip(numbers, outs):
        for group, chunks in enumerate(groups_of(owned)):
            rows = hidden[chunks[0] * lines : (chunks[-1] + 1) * lines, :]
            value = dot(rows, down[order[group], :, features_of(m, share)]).astype(out.dtype)
            for spot, chunk in enumerate(chunks):
                out[:, chunk * share : (chunk + 1) * share] = value[spot * lines : (spot + 1) * lines]


def second_kernel(numbers, out_number, info, gate, up, down, gate_in, up_in, *refs):
    *blocks, hidden, out = refs
    order = order_of(info, gate.shape[0])
    for place, gate_value, up_value in projections(order, numbers, blocks, gate, up):
        gate_value = gate_value + gate_in[place, :]
        up_value = up_value + up_in[place, :]
        hidden[place, :] = (jax.nn.silu(gate_value) * up_value).astype(BF16)
    down_parts(order, [out_number], hidden, down, [out])


def down_kernel(numbers, info, down, hidden, *outs):
    down_parts(order_of(info, down.shape[0]), numbers, hidden, down, outs)


def mixed_part(mixtures, pieces, columns):
    share = next(iter(pieces.values())).shape[1] // mixtures.shape[0]
    weights, rows = [], []
    for chunk in range(mixtures.shape[0]):
        for n, piece in pieces.items():
            size = piece.shape[0]
            values = piece[:, chunk * share + columns.start : chunk * share + columns.stop]
            for half in range(2):
                weights.append(mixtures[chunk, half, n * size : (n + 1) * size, :])
                rows.append(values)
    return dot_rows(jnp.concatenate(weights, axis=0), jnp.concatenate(rows, axis=0))


def mix_kernel(places, mixtures, *refs):
    *pieces, out, result, sems = refs
    share = out.shape[1]
    middle = share // 256 * 128
    copies = []
    for n, columns in enumerate((slice(0, middle), slice(middle, share))):
        value = mixed_part(mixtures, dict(zip(places, pieces)), columns)
        result[:, columns] = value.astype(result.dtype)
        copies.append(pltpu.make_async_copy(result.at[:, columns], out.at[:, columns], sems.at[n]))
        copies[-1].start()
    for copy in copies:
        copy.wait()


def call(kernel, outs, *args, specs=None, out_specs=None, scratch=(), flops=0):
    if specs:
        args = [
            pltpu.with_memory_space_constraint(a, s.memory_space) for a, s in zip(args, specs)
        ]
    return pl.pallas_call(
        kernel,
        out_shape=outs,
        in_specs=specs or [VMEM] * len(args),
        out_specs=out_specs or [VMEM] * len(outs),
        scratch_shapes=list(scratch),
        compiler_params=pltpu.CompilerParams(vmem_limit_bytes=LIMIT),
        cost_estimate=pl.CostEstimate(flops=flops + 1000, bytes_accessed=1000, transcendentals=0),
    )(*args)


def swapped(value, axis, mask):
    count = lax.axis_size(axis)
    return lax.ppermute(value, axis, [(source, source ^ mask) for source in range(count)])


def turned(value, low_step, across):
    parts = lax.axis_size("dp")
    if not across:
        return swapped(value, "expert", low_step)
    return swapped(value, ("expert", "dp"), low_step * parts + across)


def per_device(tokens, expert_ids, gate_weights, replica_plan, w_gate, w_up, w_down):
    owners = lax.axis_size("expert")
    parts = lax.axis_size("dp")
    owned, model_width, hidden_share = w_gate.shape
    tok_rows, share = tokens.shape
    choices = expert_ids.shape[1]
    chunks = owned + 1
    lines = owners * CAP
    wide = chunks * share
    low = 1 << ((owners.bit_length() - 1) // 2)
    high = owners // low
    high_steps = list(range(high - 1, -1, -1))
    ways_in = [high_steps[:1] + high_steps[-1:], high_steps[1:-1]]
    ways_in = [group for group in ways_in if group]
    ways_out = [high_steps[: high // 2], high_steps[high // 2 :]]
    shape = jax.ShapeDtypeStruct
    piece = shape((low * CAP, wide), BF16)
    whole = shape((lines, wide), BF16)

    def lot(group):
        return shape((len(group) * CAP, wide), BF16)

    first_steps, rest_steps = high_steps[: high // 2], high_steps[high // 2 :]
    experts = owners * owned
    *pieces, info, place, weight, tokens_here = call(
        functools.partial(route_kernel, owned, low, first_steps),
        [piece] * len(first_steps)
        + [shape((8, 128), jnp.int32)]
        + [shape((experts, tok_rows), kind) for kind in (jnp.int32, F32)]
        + [shape(tokens.shape, BF16)],
        replica_plan, expert_ids.T, gate_weights.T, tokens,
        specs=[HBM] * 4,
        scratch=[
            pltpu.SMEM((owners,), jnp.int32),
            pltpu.VMEM((choices, tok_rows), jnp.int32),
            pltpu.VMEM((choices, tok_rows), F32),
            pltpu.SemaphoreType.DMA((4,)),
        ],
        flops=10**10,
    )
    *others, mixtures = call(
        functools.partial(rest_kernel, owned, low, rest_steps, high_steps),
        [piece] * len(rest_steps) + [shape((chunks, 2, lines, tok_rows), BF16)],
        place, weight, tokens_here,
    )
    pieces += others
    arrived = {k: swapped(p, "expert", k * low) if k else p for k, p in zip(high_steps, pieces)}

    top = parts // 2
    rows, here, there = [], [], []
    for group in ways_in:
        lots = call(
            functools.partial(regroup_kernel, len(group), [
                [(n, m) for n in range(len(group))] for m in range(low)
            ]),
            [lot(group)] * low,
            *[arrived[k] for k in group],
        )
        there += [turned(value, m, top) for m, value in enumerate(lots)]
        here += [turned(value, m, 0) if m else value for m, value in enumerate(lots)]
        rows += [(k, m) for m in range(low) for k in group]
    moves = [(n, b) for n, value in enumerate(here) for b in range(value.shape[0] // CAP)]
    there, here = (
        call(functools.partial(regroup_kernel, len(lots), [moves]), [whole], *lots)[0]
        for lots in (there, here)
    )
    blocks = {top: there, 0: here}
    mask = top // 2
    while mask:
        for n in list(blocks):
            blocks[n ^ mask] = swapped(blocks[n], "dp", mask)
        mask //= 2
    first = [0, *range(top, parts)]
    second = [n for n in range(parts) if n not in first]
    sums = [shape((chunks * lines, hidden_share), F32)] * 2
    gate_sum, up_sum = call(
        functools.partial(first_kernel, first),
        sums,
        info, w_gate, w_up, w_down, *[blocks[n] for n in first],
    )
    outs = {}
    hidden, outs[parts - 1] = call(
        functools.partial(second_kernel, second, parts - 1),
        [shape((chunks * lines, hidden_share), BF16), whole],
        info, w_gate, w_up, w_down, gate_sum, up_sum, *[blocks[n] for n in second],
    )
    far, near = list(range(top, parts - 1)), list(range(top))
    for numbers in (far, near):
        found = call(
            functools.partial(down_kernel, numbers), [whole] * len(numbers), info, w_down, hidden
        )
        outs |= dict(zip(numbers, found))

    def reduced(begin):
        found = {n: outs[n] for n in range(begin, begin + top)}
        mask = 1
        while 2 * mask < top:
            for n in [n for n in found if n & mask]:
                value = swapped(found.pop(n), "dp", mask)
                (found[n ^ mask],) = call(
                    functools.partial(sum_kernel, 2, [
                        [[(0, b), (1, b)] for b in range(len(rows))]
                    ]),
                    [whole], found[n ^ mask], value,
                )
            mask *= 2
        return [swapped(value, "dp", mask) if n & mask else value for n, value in found.items()]

    def summed(wanted, *terms):
        values, moves, kinds = [value for both in terms for value in both], [], []
        for group in ways_out:
            for t, steps in wanted:
                places = [t * len(terms[t]) + n for n in range(len(terms[t]))]
                for m in steps:
                    moves.append([[(n, rows.index((k, m))) for n in places] for k in group])
                    kinds.append(lot(group))
        return call(functools.partial(sum_kernel, len(values), moves), kinds, *values)

    far_terms, near_terms = reduced(top), reduced(0)
    across = summed([(0, [0])], far_terms)
    others = summed([(0, range(low)), (1, range(1, low))], near_terms, far_terms)
    lots_out = [
        [across[g], *others[g * (2 * low - 1) : (g + 1) * (2 * low - 1)]]
        for g in range(len(ways_out))
    ]
    back = {}
    for group, lots in zip(ways_out, lots_out):
        terms, near_lots, far_lots = [], lots[1 : 1 + low], [lots[0], *lots[1 + low :]]
        for m in range(low):
            terms.append(turned(near_lots[m], m, 0) if m else near_lots[m])
            terms.append(turned(far_lots[m], m, top))
        moves = [[[(2 * m, n), (2 * m + 1, n)] for m in range(low)] for n in range(len(group))]
        totals = call(
            functools.partial(sum_kernel, 2 * low, moves), [piece] * len(group), *terms
        )
        for k, value in zip(group, totals):
            back[k] = swapped(value, "expert", k * low) if k else value
    (mixed_out,) = call(
        functools.partial(mix_kernel, range(high)),
        [shape((tok_rows, share), BF16)],
        mixtures, *[back[k] for k in high_steps],
        out_specs=[HBM],
        scratch=[pltpu.VMEM((tok_rows, share), BF16), pltpu.SemaphoreType.DMA((2,))],
    )
    return mixed_out


def solution(mesh):
    in_specs = (
        P("expert", "dp"),
        P("expert", None),
        P("expert", None),
        P(),
        P("expert", None, "dp"),
        P("expert", None, "dp"),
        P("expert", "dp", None),
    )
    out_specs = P("expert", "dp")
    return jax.shard_map(
        per_device, mesh=mesh, in_specs=in_specs, out_specs=out_specs, check_vma=False
    )
```
